32 devices in a mesh: wide: 8 (over z, y), narrow: 4 (over x, core).
Axes of the slice: x: 2, y: 2, z: 4, core: 2. Of those that a mesh axis runs over, the one named last changes fastest.
Arguments:
- tokens: bfloat16 [4096, 1024], P('wide'), may hold values from -1.5 to 1.5
- w_qk1: bfloat16 [1024, 1024], P(None, 'narrow')
- w_value1: bfloat16 [1024, 1024], P(None, 'narrow'), may hold values from -0.1875 to 0.1875
- w_out1: bfloat16 [1024, 1024], P('narrow'), may hold values from -0.1875 to 0.1875
- w_qk2: bfloat16 [1024, 1024], P(None, 'narrow')
- w_value2: bfloat16 [1024, 1024], P(None, 'narrow'), may hold values from -0.1875 to 0.1875
- w_out2: bfloat16 [1024, 1024], P('narrow'), may hold values from -0.5 to 0.5
- cluster_ids: int32 [8, 4096], P('narrow', 'wide'), may hold values from 0 to 3, as said below
Outputs:
- layer_out: float32 [4096, 1024], P('wide', 'narrow')
The draws below stay inside these ranges and needn't reach their ends.
Inputs may be any that keep to these rules, and one draw needn't show every extreme that they name: `cluster_ids`: within the 512 tokens of one index of wide, for each head, a quarter of the clusters hold 256 tokens each, half hold 96 and a quarter hold 64; which clusters are which is the same in every such block of one head.
All inputs are finite; a program needn't handle non-finite values.
Results may differ from the reference program's by a relative error of at most 0.022.
Values may be sent and summed in bfloat16 or wider, within the bound.
A program may use at most 64 MiB of HBM per device.

```python
import math
import jax
import jax.numpy as jnp
from jax import lax

D = 1024
HEADS = 8
HEAD_DIM = 128
WINDOW = 256
TOK_DEV = 512
SEQ = 4096
NCLUS = 4
CAP = 256
N_WIDE = 8
N_NARROW = 4


def scaled_normal(key, factor):
    values = jax.random.normal(key, (D, D), jnp.float32) * (factor / math.sqrt(D))
    return values.astype(jnp.bfloat16)


def draw_w_qk1(key, part):
    key = jax.random.fold_in(key, 11)
    return scaled_normal(key, 0.5)


def draw_w_qk2(key, part):
    key = jax.random.fold_in(key, 13)
    return scaled_normal(key, 0.5)


def draw_cluster_ids(key, part):
    key = jax.random.fold_in(key, 21)
    blocks = SEQ // TOK_DEV
    quarter = NCLUS // 4
    ranks = jnp.arange(NCLUS, dtype=jnp.int32)
    quota = jnp.where(ranks < quarter, CAP, jnp.where(ranks < 3 * quarter, 3 * CAP // 8, CAP // 4))
    ends = jnp.cumsum(quota)
    places = jnp.arange(TOK_DEV, dtype=jnp.int32)
    rank_of_place = jnp.sum((ends[:, None] <= places[None, :]).astype(jnp.int32), axis=0)

    def one_head(head_key):
        order_key, block_key = jax.random.split(head_key)
        order = jax.random.permutation(order_key, NCLUS)
        labels = order[rank_of_place]
        shuffles = jax.vmap(lambda item: jax.random.permutation(item, TOK_DEV))(jax.random.split(block_key, blocks))
        return labels[shuffles].reshape(SEQ)
    return jax.vmap(one_head)(jax.random.split(key, HEADS)).astype(jnp.int32)


def steps_of(own_key, shape, shards, low, top_value):
    factor_of, own = 1.0, jax.random.fold_in(own_key, 6)
    for dim, shards_of in shards:
        heights = jnp.exp(jax.random.uniform(jax.random.fold_in(own, dim), (shards_of,), jnp.float32, low / len(shards), top_value / len(shards)))
        factor_of = factor_of * jnp.repeat(heights, shape[dim] // shards_of).reshape([-1 if axis == dim else 1 for axis in range(len(shape))])
    return factor_of


def scatter_about(own_key, dims, spread, most, cuts=(), kind=jnp.bfloat16):
    result = jax.random.normal(own_key, dims, jnp.float32) * spread
    if len(cuts) > 0:
        result = steps_of(own_key, dims, cuts, -0.22, 0.18) * result
    return jnp.clip(result, min=-most, max=most).astype(kind)


def setup_inputs(seed: int = 0) -> dict:
    splits = jax.random.split(jax.random.key(seed), 9)
    tokens = scatter_about(splits[0], (SEQ, D), 0.25, 1.5, ((0, 8),))
    w_qk1 = draw_w_qk1(jax.random.fold_in(splits[8], 71), 0)
    w_value1 = scatter_about(splits[2], (D, D), D ** -0.5, 0.1875, ((1, 4),))
    w_out1 = scatter_about(splits[3], (D, D), D ** -0.5, 0.1875, ((0, 4),))
    w_qk2 = draw_w_qk2(jax.random.fold_in(splits[8], 71), 0)
    w_value2 = scatter_about(splits[5], (D, D), D ** -0.5, 0.1875, ((1, 4),))
    w_out2 = scatter_about(splits[6], (D, D), HEAD_DIM ** -0.5, 0.5, ((0, 4),))
    cluster_ids = draw_cluster_ids(jax.random.fold_in(splits[8], 71), 0)
    return dict(tokens=tokens, w_qk1=w_qk1, w_value1=w_value1, w_out1=w_out1, w_qk2=w_qk2, w_value2=w_value2, w_out2=w_out2, cluster_ids=cluster_ids)


EPS = 1e-06

def rms_round(rows):
    values = rows.astype(jnp.float32)
    factor = lax.rsqrt(lax.optimization_barrier(jnp.mean(values * values, axis=-1, keepdims=True)) + EPS)
    return (values * factor).astype(jnp.bfloat16)

def project(normed, weight):
    return jnp.dot(normed, weight, preferred_element_type=jnp.float32).astype(jnp.bfloat16)

def window_attention(query, keys, values):
    length = query.shape[0]
    block = min(512, length)
    heads = query.shape[1] // HEAD_DIM
    factor = 1.0 / math.sqrt(HEAD_DIM)

    def one_block(start):
        q = lax.dynamic_slice_in_dim(query, start, block, 0).reshape(block, heads, HEAD_DIM).astype(jnp.float32)
        k = lax.dynamic_slice_in_dim(keys, start, block + WINDOW, 0).reshape(block + WINDOW, heads, HEAD_DIM).astype(jnp.float32)
        v = lax.dynamic_slice_in_dim(values, start, block + WINDOW, 0).reshape(block + WINDOW, heads, HEAD_DIM).astype(jnp.float32)
        scores = jnp.einsum('qhd,khd->hqk', q, k, precision=lax.Precision.HIGHEST) * factor
        qpos = start + jnp.arange(block, dtype=jnp.int32)
        kpos = start - WINDOW + jnp.arange(block + WINDOW, dtype=jnp.int32)
        gap = qpos[:, None] - kpos[None, :]
        keep = (gap > 0) & (gap < WINDOW) & (kpos[None, :] >= 0) | (gap == 0) & (qpos[:, None] == 0)
        scores = jnp.where(keep[None], scores, -1e+30)
        top = lax.optimization_barrier(jnp.max(scores, axis=-1, keepdims=True))
        weights = jnp.exp(scores - top)
        totals = lax.optimization_barrier(jnp.sum(weights, axis=-1))
        rounded = weights.astype(jnp.bfloat16).astype(jnp.float32)
        mixed = jnp.einsum('hqk,khd->qhd', rounded, v, precision=lax.Precision.HIGHEST)
        mixed = mixed / jnp.transpose(totals)[:, :, None]
        return mixed.reshape(block, heads * HEAD_DIM).astype(jnp.bfloat16)
    starts = jnp.arange(length // block, dtype=jnp.int32) * block
    return lax.map(one_block, starts).reshape(length, heads * HEAD_DIM)

def grouped_sum(mixed, weight):
    step = D // N_NARROW
    total = jnp.zeros((mixed.shape[0], D), jnp.float32)
    for group in range(N_NARROW):
        term = jnp.dot(mixed[:, group * step:(group + 1) * step], weight[group * step:(group + 1) * step], preferred_element_type=jnp.float32)
        total = total + term.astype(jnp.bfloat16).astype(jnp.float32)
    return total

def cluster_attention(shared, values, labels):
    most = N_WIDE * CAP
    block = min(512, most)
    factor = 1.0 / math.sqrt(HEAD_DIM)
    match = labels[:, None] == jnp.arange(NCLUS, dtype=jnp.int32)[None, :]
    running = jnp.cumsum(match.astype(jnp.int32), axis=0)
    rank = (lax.optimization_barrier(jnp.sum(jnp.where(match, running, 0), axis=1)) - 1).astype(jnp.int32)
    table = jnp.full((NCLUS, most), SEQ, jnp.int32).at[labels, rank].set(jnp.arange(SEQ, dtype=jnp.int32))
    order = jnp.arange(most, dtype=jnp.int32)

    def one_cluster(members):
        live = members < SEQ
        safe = jnp.minimum(members, SEQ - 1)
        kc = shared[safe].astype(jnp.float32)
        vc = values[safe].astype(jnp.float32)

        def one_block(start):
            q = lax.dynamic_slice_in_dim(kc, start, block, 0)
            scores = jnp.dot(q, kc.T, precision=lax.Precision.HIGHEST) * factor
            rows_here = start + jnp.arange(block, dtype=jnp.int32)
            earlier = order[None, :] < rows_here[:, None]
            alone = (order[None, :] == rows_here[:, None]) & (rows_here[:, None] == 0)
            keep = (earlier | alone) & live[None, :]
            scores = jnp.where(keep, scores, -1e+30)
            top = lax.optimization_barrier(jnp.max(scores, axis=-1, keepdims=True))
            weights = jnp.exp(scores - top)
            totals = lax.optimization_barrier(jnp.sum(weights, axis=-1))
            rounded = weights.astype(jnp.bfloat16).astype(jnp.float32)
            mixed = jnp.dot(rounded, vc, precision=lax.Precision.HIGHEST) / totals[:, None]
            return mixed.astype(jnp.bfloat16)
        starts = jnp.arange(most // block, dtype=jnp.int32) * block
        return lax.map(one_block, starts).reshape(most, HEAD_DIM)
    results = lax.map(one_cluster, table)
    placed = jnp.zeros((SEQ, HEAD_DIM), jnp.bfloat16)
    return placed.at[table.reshape(-1)].set(results.reshape(-1, HEAD_DIM), mode='drop')

def reference(tokens, w_qk1, w_value1, w_out1, w_qk2, w_value2, w_out2, cluster_ids):
    normed = rms_round(tokens)
    qk1 = project(normed, w_qk1)
    value1 = project(normed, w_value1)
    padding = jnp.zeros((WINDOW, D), jnp.bfloat16)
    attended1 = window_attention(qk1, jnp.concatenate([padding, qk1], axis=0), jnp.concatenate([padding, value1], axis=0))
    hidden = (tokens.astype(jnp.float32) + grouped_sum(attended1, w_out1)).astype(jnp.bfloat16)
    normed2 = rms_round(hidden)
    qk2 = project(normed2, w_qk2)
    value2 = project(normed2, w_value2)
    outputs = []
    for head in range(HEADS):
        cols = slice(head * HEAD_DIM, (head + 1) * HEAD_DIM)
        outputs.append(cluster_attention(qk2[:, cols], value2[:, cols], cluster_ids[head]))
    attended2 = jnp.concatenate(outputs, axis=1)
    return hidden.astype(jnp.float32) + grouped_sum(attended2, w_out2)
```

```python
import functools
import math

import jax
import jax.numpy as jnp
from jax import lax
from jax.experimental import pallas as pl
from jax.experimental.pallas import tpu as pltpu
from jax.sharding import PartitionSpec as P

HEAD_DIM = 128
WINDOW = 256
EPS = 1e-06
BLOCK = 256
SCALE = math.log2(math.e) / math.sqrt(HEAD_DIM)
LOW = -1e30
MESH = pl.DeviceIdType.MESH
F32 = jnp.float32
BF16 = jnp.bfloat16


def flip(index, bit):
    return index + bit - 2 * bit * lax.rem(lax.div(index, bit), 2)


def rms_round(rows):
    values = rows.astype(F32)
    factor = lax.rsqrt(jnp.mean(values * values, axis=-1, keepdims=True) + EPS)
    return (values * factor).astype(BF16)


def dot(a, b):
    return jnp.dot(a, b, preferred_element_type=F32)


def dot_nt(a, b):
    return lax.dot_general(a, b, (((1,), (1,)), ((), ())), preferred_element_type=F32)


def dot_tn(a, b):
    return lax.dot_general(a, b, (((0,), (0,)), ((), ())), preferred_element_type=F32)


def send(src, dst, send_sem, recv_sem, **where):
    return pltpu.make_async_remote_copy(
        src_ref=src, dst_ref=dst, send_sem=send_sem, recv_sem=recv_sem,
        device_id=where, device_id_type=MESH)


def whole_kernel(wide_n, heads, clusters, sizes, pads, slots,
                 tokens, w_qk1, w_value1, w_out1, w_qk2, w_value2, w_out2, ids, out,
                 kvx, w1, att1, hidden, kv2, to_slot, to_token, packed, arrived, answers, ret, att2, w2,
                 halo_sem, w1_sems, att1_sems, w2_sems, go_s, go_r, back_s, back_r, att2_sems, local_sem):
    me, n = lax.axis_index("wide"), lax.axis_index("narrow")
    near, far = flip(n, 1), flip(n, 2)
    cross = flip(near, 2)
    length = tokens.shape[0]
    cols = w_qk1.shape[1]
    counts = (clusters // 4, clusters // 2, clusters // 4)
    starts = (0, clusters // 4, 3 * clusters // 4)
    bases = (0, counts[0] * pads[0], counts[0] * pads[0] + counts[1] * pads[1])
    core = lax.rem(n, 2)

    def shuffle(place):
        low = flip(place, 2)
        high = flip(place, 1)
        return jnp.where(place < wide_n // 2, low, high)

    def flip_core(place):
        return jnp.where(core == 1, flip(place, 1), place)

    def device_of(owner):
        return flip_core(shuffle(owner))

    mine = shuffle(flip_core(me))
    my_head, my_rank = lax.div(mine, clusters), lax.rem(mine, clusters)

    barrier = pltpu.get_barrier_semaphore()

    @pl.loop(1, wide_n)
    def _(k):
        pl.semaphore_signal(barrier, inc=1, device_id={"wide": lax.rem(me + k, wide_n)}, device_id_type=MESH)

    for other in (near, far, cross):
        pl.semaphore_signal(barrier, inc=1, device_id={"narrow": other}, device_id_type=MESH)
    pl.semaphore_wait(barrier, wide_n - 1 + 3)

    w1_far = send(w_out1, w1.at[n], w1_sems.at[0, 0], w1_sems.at[1, 0], narrow=far)
    w1_near = send(w_out1, w1.at[n], w1_sems.at[0, 1], w1_sems.at[1, 1], narrow=near)
    w1_fwd = send(w1.at[far], w1.at[far], w1_sems.at[0, 2], w1_sems.at[1, 2], narrow=near)
    w1_far.start()
    w1_near.start()

    def project1(start):
        rows = pl.ds(start, BLOCK)
        normed = rms_round(tokens[rows, :])
        there = pl.ds(WINDOW + start, BLOCK)
        kvx[there, pl.ds(0, cols)] = dot(normed, w_qk1[...]).astype(BF16)
        kvx[there, pl.ds(cols, cols)] = dot(normed, w_value1[...]).astype(BF16)

    tail = length - BLOCK
    halo = send(kvx.at[pl.ds(length, WINDOW)], kvx.at[pl.ds(0, WINDOW)], halo_sem.at[0], halo_sem.at[1],
                wide=lax.rem(me + 1, wide_n))
    project1(tail)

    @pl.when(me < wide_n - 1)
    def _():
        halo.start()

    @pl.when(me == 0)
    def _():
        kvx[pl.ds(0, WINDOW), :] = jnp.zeros((WINDOW, 2 * cols), BF16)

    project1(0)

    def window(start):
        key_at = lax.broadcasted_iota(jnp.int32, (2 * BLOCK, BLOCK), 0) + (me * length + start - WINDOW)
        query_at = lax.broadcasted_iota(jnp.int32, (2 * BLOCK, BLOCK), 1) + (me * length + start)
        gap = query_at - key_at
        keep = (gap > 0) & (gap < WINDOW) & (key_at >= 0) | (gap == 0) & (query_at == 0)
        for h in range(heads):
            q = kvx[pl.ds(start + WINDOW, BLOCK), pl.ds(h * HEAD_DIM, HEAD_DIM)]
            k = kvx[pl.ds(start, 2 * BLOCK), pl.ds(h * HEAD_DIM, HEAD_DIM)]
            v = kvx[pl.ds(start, 2 * BLOCK), pl.ds(cols + h * HEAD_DIM, HEAD_DIM)]
            scores = jnp.where(keep, dot_nt(k, q) * SCALE, LOW)
            top = jnp.max(scores, axis=0, keepdims=True)
            weights = jnp.exp2(scores - top)
            total = jnp.sum(weights, axis=0, keepdims=True)
            mixed = dot_tn(v, weights.astype(BF16)) / total
            att1[n, pl.ds(start, BLOCK), pl.ds(h * HEAD_DIM, HEAD_DIM)] = mixed.T.astype(BF16)

    def share(buffer, sems, half):
        rows = pl.ds(half * BLOCK, BLOCK)
        first = send(buffer.at[n, rows], buffer.at[n, rows], sems.at[0, half, 0], sems.at[1, half, 0], narrow=far)
        second = send(buffer.at[n, rows], buffer.at[n, rows], sems.at[0, half, 1], sems.at[1, half, 1], narrow=near)
        third = send(buffer.at[far, rows], buffer.at[far, rows], sems.at[0, half, 2], sems.at[1, half, 2],
                     narrow=near)
        return first, second, third

    att1_sends = [share(att1, att1_sems, half) for half in range(2)]
    window(tail)
    att1_sends[1][0].start()
    att1_sends[1][1].start()

    @pl.when(me > 0)
    def _():
        halo.wait_recv()

    window(0)
    att1_sends[0][0].start()
    att1_sends[0][1].start()

    w2_sends = []
    for index, other in enumerate((near, far, cross)):
        w2_sends.append(send(w_out2.at[:, pl.ds(pl.multiple_of(other * cols, cols), cols)], w2.at[n],
                             w2_sems.at[0, index], w2_sems.at[1, index], narrow=other))
        w2_sends[-1].start()
    w2[n] = w_out2[:, pl.ds(pl.multiple_of(n * cols, cols), cols)]
    w1[n] = w_out1[...]

    most = 128
    before = (lax.broadcasted_iota(jnp.int32, (length, length), 0)
              <= lax.broadcasted_iota(jnp.int32, (length, length), 1)).astype(F32).astype(BF16)
    for h in range(heads):
        match = (lax.broadcasted_iota(jnp.int32, (most, length), 0) == ids[pl.ds(h, 1), :]).astype(F32)
        match16 = match.astype(BF16)
        running = dot(match16, before)
        held = jnp.sum(match, axis=1, keepdims=True)
        held_row = dot_nt(jnp.ones((8, length), BF16), match16)[0:1, :]
        lower = (lax.broadcasted_iota(jnp.int32, (most, most), 1)
                 < lax.broadcasted_iota(jnp.int32, (most, most), 0))
        ahead = (held_row > held) | (held_row == held) & lower
        rank = jnp.sum(ahead.astype(F32), axis=1, keepdims=True)
        base = jnp.where(
            rank < starts[1], rank * pads[0],
            jnp.where(rank < starts[2], bases[1] + (rank - starts[1]) * pads[1],
                      bases[2] + (rank - starts[2]) * pads[2]))
        target = jnp.sum(match * (base + running - 1.0), axis=0, keepdims=True)
        target_col = jnp.broadcast_to(target, (8, length)).T[:, 0:1].astype(jnp.int32)
        target = target.astype(jnp.int32)
        to_slot[h] = (lax.broadcasted_iota(jnp.int32, (slots, length), 0) == target).astype(F32).astype(BF16)
        to_token[h] = (lax.broadcasted_iota(jnp.int32, (length, slots), 1) == target_col).astype(F32).astype(BF16)

    w1_far.wait_recv()
    w1_fwd.start()
    w1_near.wait_recv()
    for half in (1, 0):
        first, second, third = att1_sends[half]
        first.wait_recv()
        third.start()
    w1_fwd.wait_recv()

    for half in (1, 0):
        first, second, third = att1_sends[half]
        second.wait_recv()
        third.wait_recv()
        rows = pl.ds(half * BLOCK, BLOCK)
        total = tokens[rows, :].astype(F32)
        for g in range(4):
            total = total + dot(att1[g, rows, :], w1[g])
        hidden16 = total.astype(BF16)
        hidden[rows, :] = hidden16
        normed = rms_round(hidden16)
        qk2 = dot(normed, w_qk2[...]).astype(BF16)
        value2 = dot(normed, w_value2[...]).astype(BF16)
        for h in range(heads):
            part = slice(h * HEAD_DIM, (h + 1) * HEAD_DIM)
            kv2[h, rows, pl.ds(0, HEAD_DIM)] = qk2[:, part]
            kv2[h, rows, pl.ds(HEAD_DIM, HEAD_DIM)] = value2[:, part]

    for h in range(heads):
        packed[h] = dot(to_slot[h], kv2[h]).astype(BF16)

    def place(level, head, step):
        rank = starts[level] + step
        owner = head * clusters + rank
        offset = pl.multiple_of(bases[level] + step * pads[level], 16)
        return owner, device_of(owner), offset

    def go(level, head, step):
        owner, there, offset = place(level, head, step)
        size = pads[level]
        return there, send(packed.at[head, pl.ds(offset, size)],
                           arrived.at[pl.ds(pl.multiple_of(me * size, 16), size)],
                           go_s.at[owner], go_r.at[me], wide=there), (head, offset, size)

    def each_owner(body):
        for level in range(3):
            @pl.loop(0, heads * counts[level])
            def _(item):
                body(level, lax.div(item, counts[level]), lax.rem(item, counts[level]))

    def start_go(level, head, step):
        there, copy, (head, offset, size) = go(level, head, step)

        @pl.when(there != me)
        def _():
            copy.start()

        @pl.when(there == me)
        def _():
            own = pltpu.make_async_copy(packed.at[head, pl.ds(offset, size)],
                                        arrived.at[pl.ds(pl.multiple_of(me * size, 16), size)], local_sem)
            own.start()
            own.wait()

    each_owner(start_go)

    def for_level(body):
        for level in range(3):
            @pl.when((my_rank >= starts[level]) & (my_rank < starts[level] + counts[level]))
            def _():
                body(level)

    def from_source(level, source):
        size = pads[level]
        rows = pl.ds(pl.multiple_of(source * size, 16), size)
        return send(packed.at[0, pl.ds(0, size)], arrived.at[rows], go_s.at[0], go_r.at[source], wide=source)

    def back_copy(level, source):
        size = pads[level]
        rows = pl.ds(pl.multiple_of(source * size, 16), size)
        offset = pl.multiple_of(bases[level] + (my_rank - starts[level]) * size, 16)
        return rows, offset, send(answers.at[rows], ret.at[my_head, pl.ds(offset, size)],
                                  back_s.at[source], back_r.at[mine], wide=source)

    def receive(level, source):
        @pl.when(source != me)
        def _():
            from_source(level, source).wait_recv()

    def give_back(level, source):
        rows, offset, copy = back_copy(level, source)

        @pl.when(source != me)
        def _():
            copy.start()

        @pl.when(source == me)
        def _():
            own = pltpu.make_async_copy(answers.at[rows], ret.at[my_head, pl.ds(offset, pads[level])], local_sem)
            own.start()
            own.wait()

    def attend(level, block):
        size, real = pads[level], sizes[level]
        here = pl.ds(pl.multiple_of(block * BLOCK, BLOCK), BLOCK)
        q = arrived[here, pl.ds(0, HEAD_DIM)]
        key_at = lax.broadcasted_iota(jnp.int32, (BLOCK, BLOCK), 0)
        query_at = lax.broadcasted_iota(jnp.int32, (BLOCK, BLOCK), 1)

        def score(rows, step, diagonal):
            scores = dot_nt(arrived[rows, pl.ds(0, HEAD_DIM)], q) * SCALE
            keep = None
            if diagonal:
                keep = (key_at < query_at) | (key_at == query_at) & (query_at + block * BLOCK == 0)
            if size != real:
                live = lax.rem(key_at + step * BLOCK, size) < real
                keep = live if keep is None else keep & live
            return scores if keep is None else jnp.where(keep, scores, LOW)

        scores = score(here, block, True)
        top = jnp.max(scores, axis=0, keepdims=True)
        weights = jnp.exp2(scores - top)
        total = jnp.sum(weights, axis=0, keepdims=True)
        mixed = dot_tn(arrived[here, pl.ds(HEAD_DIM, HEAD_DIM)], weights.astype(BF16))

        def earlier(step, carry):
            top, total, mixed = carry
            rows = pl.ds(pl.multiple_of(step * BLOCK, BLOCK), BLOCK)
            scores = score(rows, step, False)
            newer = jnp.maximum(top, jnp.max(scores, axis=0, keepdims=True))
            weights = jnp.exp2(scores - newer)
            shrink = jnp.exp2(top - newer)
            total = total * shrink + jnp.sum(weights, axis=0, keepdims=True)
            mixed = mixed * shrink + dot_tn(arrived[rows, pl.ds(HEAD_DIM, HEAD_DIM)], weights.astype(BF16))
            return newer, total, mixed

        top, total, mixed = lax.fori_loop(0, block, earlier, (top, total, mixed))
        answers[here, :] = (mixed / total).T.astype(BF16)

    def own_clusters(level):
        blocks = wide_n * pads[level] // BLOCK
        if pads[level] == BLOCK:
            @pl.loop(0, blocks)
            def _(block):
                receive(level, block)
                attend(level, block)
                give_back(level, block)
        else:
            @pl.loop(0, wide_n)
            def _(source):
                receive(level, source)

            @pl.loop(0, blocks)
            def _(block):
                attend(level, block)

            @pl.loop(0, wide_n)
            def _(source):
                give_back(level, source)

    for_level(own_clusters)

    def wait_back(level, head, step):
        owner, there, offset = place(level, head, step)
        size = pads[level]

        @pl.when(there != me)
        def _():
            send(answers.at[pl.ds(0, size)], ret.at[head, pl.ds(offset, size)],
                 back_s.at[0], back_r.at[owner], wide=there).wait_recv()

    each_owner(wait_back)
    att2_sends = [share(att2, att2_sems, half) for half in range(2)]
    for half in range(2):
        rows = pl.ds(half * BLOCK, BLOCK)
        for h in range(heads):
            att2[n, rows, pl.ds(h * HEAD_DIM, HEAD_DIM)] = dot(to_token[h, rows, :], ret[h]).astype(BF16)
        att2_sends[half][0].start()
        att2_sends[half][1].start()
    for copy in w2_sends:
        copy.wait_recv()
    for half in range(2):
        att2_sends[half][0].wait_recv()
        att2_sends[half][2].start()
    for half in range(2):
        rows = pl.ds(half * BLOCK, BLOCK)
        att2_sends[half][1].wait_recv()
        att2_sends[half][2].wait_recv()
        total = hidden[rows, pl.ds(pl.multiple_of(n * cols, cols), cols)].astype(F32)
        for g in range(4):
            total = total + dot(att2[g, rows, :], w2[g])
        out[rows, :] = total

    for copy in (w1_far, w1_near, w1_fwd, *w2_sends, *att1_sends[0], *att1_sends[1], *att2_sends[0], *att2_sends[1]):
        copy.wait_send()

    @pl.when(me < wide_n - 1)
    def _():
        halo.wait_send()

    def sent(level, head, step):
        there, copy, _ = go(level, head, step)

        @pl.when(there != me)
        def _():
            copy.wait_send()

    each_owner(sent)

    def sent_back(level):
        @pl.loop(0, wide_n)
        def _(source):
            @pl.when(source != me)
            def _():
                back_copy(level, source)[2].wait_send()

    for_level(sent_back)


def solution(mesh):
    wide_n = mesh.shape["wide"]

    def shards(tokens, w_qk1, w_value1, w_out1, w_qk2, w_value2, w_out2, cluster_ids):
        length, width = tokens.shape
        cols = w_qk1.shape[1]
        heads = cols // HEAD_DIM
        clusters = wide_n // heads
        cap = 2 * length * heads // wide_n
        sizes = (cap, 3 * cap // 8, cap // 4)
        pads = tuple(-(-size // 16) * 16 for size in sizes)
        slots = clusters // 4 * pads[0] + clusters // 2 * pads[1] + clusters // 4 * pads[2]
        most = wide_n * pads[0]
        groups = mesh.shape["narrow"]
        dma = pltpu.SemaphoreType.DMA
        vmem = pl.BlockSpec(memory_space=pltpu.VMEM)
        return pl.pallas_call(
            functools.partial(whole_kernel, wide_n, heads, clusters, sizes, pads, slots),
            out_shape=jax.ShapeDtypeStruct((length, cols), F32),
            in_specs=[vmem] * 8,
            out_specs=vmem,
            scratch_shapes=[
                pltpu.VMEM((WINDOW + length, 2 * cols), BF16),
                pltpu.VMEM((groups, cols, width), BF16),
                pltpu.VMEM((groups, length, cols), BF16),
                pltpu.VMEM((length, width), BF16),
                pltpu.VMEM((heads, length, 2 * HEAD_DIM), BF16),
                pltpu.VMEM((heads, slots, length), BF16),
                pltpu.VMEM((heads, length, slots), BF16),
                pltpu.VMEM((heads, slots, 2 * HEAD_DIM), BF16),
                pltpu.VMEM((most, 2 * HEAD_DIM), BF16),
                pltpu.VMEM((most, HEAD_DIM), BF16),
                pltpu.VMEM((heads, slots, HEAD_DIM), BF16),
                pltpu.VMEM((groups, length, cols), BF16),
                pltpu.VMEM((groups, cols, cols), BF16),
                dma((2,)), dma((2, 3)), dma((2, 2, 3)), dma((2, 3)),
                dma((wide_n,)), dma((wide_n,)), dma((wide_n,)), dma((wide_n,)),
                dma((2, 2, 3)), dma,
            ],
            compiler_params=pltpu.CompilerParams(
                collective_id=0, has_side_effects=True, vmem_limit_bytes=56 * 1024 * 1024),
        )(tokens, w_qk1, w_value1, w_out1, w_qk2, w_value2, w_out2, cluster_ids)

    placed = (
        P("wide", None),
        P(None, "narrow"),
        P(None, "narrow"),
        P("narrow", None),
        P(None, "narrow"),
        P(None, "narrow"),
        P("narrow", None),
        P("narrow", "wide"),
    )
    return jax.shard_map(
        shards, mesh=mesh, in_specs=placed, out_specs=P("wide", "narrow"), check_vma=False
    )
```

```python
import functools
import math

import jax
import jax.numpy as jnp
from jax import lax
from jax.experimental import pallas as pl
from jax.experimental.pallas import tpu as pltpu
from jax.sharding import PartitionSpec as P

HEAD_DIM = 128
WINDOW = 256
EPS = 1e-06
BLOCK = 256
SCALE = math.log2(math.e) / math.sqrt(HEAD_DIM)
LOW = -1e30
MESH = pl.DeviceIdType.MESH
F32 = jnp.float32
BF16 = jnp.bfloat16


def flip(index, bit):
    return index + bit - 2 * bit * lax.rem(lax.div(index, bit), 2)


def rms_round(rows):
    values = rows.astype(F32)
    factor = lax.rsqrt(jnp.mean(values * values, axis=-1, keepdims=True) + EPS)
    return (values * factor).astype(BF16)


def dot(a, b):
    return jnp.dot(a, b, preferred_element_type=F32)


def dot_nt(a, b):
    return lax.dot_general(a, b, (((1,), (1,)), ((), ())), preferred_element_type=F32)


def dot_tn(a, b):
    return lax.dot_general(a, b, (((0,), (0,)), ((), ())), preferred_element_type=F32)


def send(src, dst, send_sem, recv_sem, **where):
    return pltpu.make_async_remote_copy(
        src_ref=src, dst_ref=dst, send_sem=send_sem, recv_sem=recv_sem,
        device_id=where, device_id_type=MESH)


def whole_kernel(wide_n, heads, clusters, sizes, pads, slots,
                 tokens, w_qk1, w_value1, w_out1, w_qk2, w_value2, w_out2, ids, out,
                 kvx, w1, att1, hidden, normed2, to_slot, to_token, packed, arrived, value_t, answers, ret, att2, w2,
                 halo_sem, w1_sems, att1_sems, w2_sems, go_s, go_r, back_s, back_r, att2_sems, local_sem):
    me, n = lax.axis_index("wide"), lax.axis_index("narrow")
    near, far = flip(n, 1), flip(n, 2)
    cross = flip(near, 2)
    length = tokens.shape[0]
    cols = w_qk1.shape[1]
    counts = (clusters // 4, clusters // 2, clusters // 4)
    starts = (0, clusters // 4, 3 * clusters // 4)
    bases = (0, counts[0] * pads[0], counts[0] * pads[0] + counts[1] * pads[1])
    core = lax.rem(n, 2)

    def shuffle(place):
        low = flip(place, 2)
        high = flip(place, 1)
        return jnp.where(place < wide_n // 2, low, high)

    def flip_core(place):
        return jnp.where(core == 1, flip(place, 1), place)

    def device_of(owner):
        return flip_core(shuffle(owner))

    mine = shuffle(flip_core(me))
    my_head, my_rank = lax.div(mine, clusters), lax.rem(mine, clusters)

    barrier = pltpu.get_barrier_semaphore()

    @pl.loop(1, wide_n)
    def _(k):
        pl.semaphore_signal(barrier, inc=1, device_id={"wide": lax.rem(me + k, wide_n)}, device_id_type=MESH)

    for other in (near, far, cross):
        pl.semaphore_signal(barrier, inc=1, device_id={"narrow": other}, device_id_type=MESH)

    def project1(start):
        rows = pl.ds(start, BLOCK)
        normed = rms_round(tokens[rows, :])
        there = pl.ds(WINDOW + start, BLOCK)
        kvx[there, pl.ds(0, cols)] = dot(normed, w_qk1[...]).astype(BF16)
        kvx[there, pl.ds(cols, cols)] = dot(normed, w_value1[...]).astype(BF16)

    tail = length - BLOCK
    half_rows = cols // 2
    beside = flip(me, 2)
    parity = lax.rem(lax.div(me, 2), 2)
    early = pl.ds(pl.multiple_of(parity * half_rows, half_rows), half_rows)
    late = pl.ds(pl.multiple_of((1 - parity) * half_rows, half_rows), half_rows)
    w1_far = send(w_out1.at[early], w1.at[n, early], w1_sems.at[0, 0], w1_sems.at[1, 0], narrow=far)
    w1_near = send(w_out1, w1.at[n], w1_sems.at[0, 1], w1_sems.at[1, 1], narrow=near)
    w1_swap = send(w1.at[far, early], w1.at[far, early], w1_sems.at[0, 2], w1_sems.at[1, 2], wide=beside)
    w1_fwd = (send(w1.at[far, early], w1.at[far, early], w1_sems.at[0, 3], w1_sems.at[1, 3], narrow=near),
              send(w1.at[far, late], w1.at[far, late], w1_sems.at[0, 4], w1_sems.at[1, 4], narrow=near))
    halo = send(kvx.at[pl.ds(length, WINDOW)], kvx.at[pl.ds(0, WINDOW)], halo_sem.at[0], halo_sem.at[1],
                wide=lax.rem(me + 1, wide_n))
    project1(tail)
    pl.semaphore_wait(barrier, wide_n - 1 + 3)
    w1_far.start()

    @pl.when(me < wide_n - 1)
    def _():
        halo.start()

    w1_near.start()

    @pl.when(me == 0)
    def _():
        kvx[pl.ds(0, WINDOW), :] = jnp.zeros((WINDOW, 2 * cols), BF16)

    project1(0)

    def window(start):
        key_at = lax.broadcasted_iota(jnp.int32, (2 * BLOCK, BLOCK), 0) + (me * length + start - WINDOW)
        query_at = lax.broadcasted_iota(jnp.int32, (2 * BLOCK, BLOCK), 1) + (me * length + start)
        gap = query_at - key_at
        keep = (gap > 0) & (gap < WINDOW) & (key_at >= 0) | (gap == 0) & (query_at == 0)
        for h in range(heads):
            q = kvx[pl.ds(start + WINDOW, BLOCK), pl.ds(h * HEAD_DIM, HEAD_DIM)]
            k = kvx[pl.ds(start, 2 * BLOCK), pl.ds(h * HEAD_DIM, HEAD_DIM)]
            v = kvx[pl.ds(start, 2 * BLOCK), pl.ds(cols + h * HEAD_DIM, HEAD_DIM)]
            scores = jnp.where(keep, dot_nt(k, q) * SCALE, LOW)
            top = jnp.max(scores, axis=0, keepdims=True)
            weights = jnp.exp2(scores - top)
            total = jnp.sum(weights, axis=0, keepdims=True)
            mixed = dot_tn(v, weights.astype(BF16)) / total
            att1[n, pl.ds(start, BLOCK), pl.ds(h * HEAD_DIM, HEAD_DIM)] = mixed.T.astype(BF16)

    def share(buffer, sems, half):
        rows = pl.ds(half * BLOCK, BLOCK)
        first = send(buffer.at[n, rows], buffer.at[n, rows], sems.at[0, half, 0], sems.at[1, half, 0], narrow=far)
        second = send(buffer.at[n, rows], buffer.at[n, rows], sems.at[0, half, 1], sems.at[1, half, 1], narrow=near)
        third = send(buffer.at[far, rows], buffer.at[far, rows], sems.at[0, half, 2], sems.at[1, half, 2],
                     narrow=near)
        return first, second, third

    att1_sends = [share(att1, att1_sems, half) for half in range(2)]
    window(tail)
    att1_sends[1][0].start()
    att1_sends[1][1].start()
    w1_far.wait_recv()
    w1_swap.start()
    w1_fwd[0].start()

    @pl.when(me > 0)
    def _():
        halo.wait_recv()

    window(0)
    att1_sends[0][0].start()
    att1_sends[0][1].start()

    w1[n] = w_out1[...]

    most = 128
    before = (lax.broadcasted_iota(jnp.int32, (length, length), 0)
              <= lax.broadcasted_iota(jnp.int32, (length, length), 1)).astype(F32).astype(BF16)
    for h in range(heads):
        match = (lax.broadcasted_iota(jnp.int32, (most, length), 0) == ids[pl.ds(h, 1), :]).astype(F32)
        match16 = match.astype(BF16)
        running = dot(match16, before)
        held = jnp.sum(match, axis=1, keepdims=True)
        held_row = dot_nt(jnp.ones((8, length), BF16), match16)[0:1, :]
        lower = (lax.broadcasted_iota(jnp.int32, (most, most), 1)
                 < lax.broadcasted_iota(jnp.int32, (most, most), 0))
        ahead = (held_row > held) | (held_row == held) & lower
        rank = jnp.sum(ahead.astype(F32), axis=1, keepdims=True)
        base = jnp.where(
            rank < starts[1], rank * pads[0],
            jnp.where(rank < starts[2], bases[1] + (rank - starts[1]) * pads[1],
                      bases[2] + (rank - starts[2]) * pads[2]))
        target = jnp.sum(match * (base + running - 1.0), axis=0, keepdims=True)
        target_col = jnp.broadcast_to(target, (8, length)).T[:, 0:1].astype(jnp.int32)
        target = target.astype(jnp.int32)
        to_slot[h] = (lax.broadcasted_iota(jnp.int32, (slots, length), 0) == target).astype(F32).astype(BF16)
        to_token[h] = (lax.broadcasted_iota(jnp.int32, (length, slots), 1) == target_col).astype(F32).astype(BF16)

    att1_sends[1][0].wait_recv()
    att1_sends[1][2].start()
    w1_swap.wait_recv()
    w1_fwd[1].start()
    att1_sends[0][0].wait_recv()
    att1_sends[0][2].start()
    w1_near.wait_recv()
    w1_fwd[0].wait_recv()
    w1_fwd[1].wait_recv()

    for half in (1, 0):
        first, second, third = att1_sends[half]
        second.wait_recv()
        third.wait_recv()
        rows = pl.ds(half * BLOCK, BLOCK)
        total = tokens[rows, :].astype(F32)
        for g in range(4):
            total = total + dot(att1[g, rows, :], w1[g])
        hidden16 = total.astype(BF16)
        hidden[rows, :] = hidden16
        normed2[rows, :] = rms_round(hidden16)

    def place(level, head, step):
        rank = starts[level] + step
        owner = head * clusters + rank
        offset = pl.multiple_of(bases[level] + step * pads[level], 16)
        return owner, device_of(owner), offset

    def go(level, head, step):
        owner, there, offset = place(level, head, step)
        size = pads[level]
        return there, send(packed.at[head, pl.ds(offset, size)],
                           arrived.at[pl.ds(pl.multiple_of(me * size, 16), size)],
                           go_s.at[owner], go_r.at[me], wide=there), (head, offset, size)

    def each_owner(body):
        for level in range(3):
            @pl.loop(0, heads * counts[level])
            def _(item):
                body(level, lax.div(item, counts[level]), lax.rem(item, counts[level]))

    def start_go(level, head, step):
        there, copy, (_, offset, size) = go(level, head, step)

        @pl.when(there != me)
        def _():
            copy.start()

        @pl.when(there == me)
        def _():
            own = pltpu.make_async_copy(packed.at[head, pl.ds(offset, size)],
                                        arrived.at[pl.ds(pl.multiple_of(me * size, 16), size)], local_sem)
            own.start()
            own.wait()

    for h in range(heads):
        part = pl.ds(h * HEAD_DIM, HEAD_DIM)
        both = jnp.concatenate([w_qk2[:, part], w_value2[:, part]], axis=1)
        packed[h] = dot(to_slot[h], dot(normed2[...], both).astype(BF16)).astype(BF16)
        for level in range(3):
            @pl.loop(0, counts[level])
            def _(step):
                start_go(level, h, step)

    w2_sends = []
    for index, other in enumerate((near, far, cross)):
        w2_sends.append(send(w_out2.at[:, pl.ds(pl.multiple_of(other * cols, cols), cols)], w2.at[n],
                             w2_sems.at[0, index], w2_sems.at[1, index], narrow=other))
        w2_sends[-1].start()
    w2[n] = w_out2[:, pl.ds(pl.multiple_of(n * cols, cols), cols)]

    def for_level(body):
        for level in range(3):
            @pl.when((my_rank >= starts[level]) & (my_rank < starts[level] + counts[level]))
            def _():
                body(level)

    def from_source(level, source):
        size = pads[level]
        rows = pl.ds(pl.multiple_of(source * size, 16), size)
        return send(packed.at[0, pl.ds(0, size)], arrived.at[rows], go_s.at[0], go_r.at[source], wide=source)

    def back_copy(level, source):
        size = pads[level]
        rows = pl.ds(pl.multiple_of(source * size, 16), size)
        offset = pl.multiple_of(bases[level] + (my_rank - starts[level]) * size, 16)
        return rows, offset, send(answers.at[rows], ret.at[my_head, pl.ds(offset, size)],
                                  back_s.at[source], back_r.at[mine], wide=source)

    def receive(level, source):
        @pl.when(source != me)
        def _():
            from_source(level, source).wait_recv()

    def give_back(level, source):
        rows, offset, copy = back_copy(level, source)

        @pl.when(source != me)
        def _():
            copy.start()

        @pl.when(source == me)
        def _():
            own = pltpu.make_async_copy(answers.at[rows], ret.at[my_head, pl.ds(offset, pads[level])], local_sem)
            own.start()
            own.wait()

    def attend(level, block):
        size, real = pads[level], sizes[level]
        begin = block * BLOCK
        here = pl.ds(begin, BLOCK)
        q = arrived[here, pl.ds(0, HEAD_DIM)]
        value_t[:, here] = arrived[here, pl.ds(HEAD_DIM, HEAD_DIM)].T

        def score(first, rows, diagonal):
            scores = dot_nt(arrived[pl.ds(first, rows), pl.ds(0, HEAD_DIM)], q) * SCALE
            keep = None
            key_at = lax.broadcasted_iota(jnp.int32, (rows, BLOCK), 0)
            if diagonal:
                query_at = lax.broadcasted_iota(jnp.int32, (rows, BLOCK), 1)
                keep = key_at < query_at
                if block == 0:
                    keep = keep | (key_at + query_at == 0)
            if size != real:
                live = lax.rem(key_at + first, size) < real
                keep = live if keep is None else keep & live
            return scores if keep is None else jnp.where(keep, scores, LOW)

        parts = [(begin, score(begin, BLOCK, True))]
        if block > 0:
            parts.append((0, score(0, begin, False)))
        top = functools.reduce(jnp.maximum, [jnp.max(scores, axis=0, keepdims=True) for _, scores in parts])
        total, mixed = 0.0, 0.0
        for first, scores in parts:
            weights = jnp.exp2(scores - top)
            total = total + jnp.sum(weights, axis=0, keepdims=True)
            mixed = mixed + dot(value_t[:, pl.ds(first, scores.shape[0])], weights.astype(BF16))
        answers[here, :] = (mixed / total).T.astype(BF16)

    def own_clusters(level):
        blocks = wide_n * pads[level] // BLOCK
        if pads[level] == BLOCK:
            for block in range(blocks):
                receive(level, block)
                attend(level, block)
                give_back(level, block)
        else:
            @pl.loop(0, wide_n)
            def _(source):
                receive(level, source)

            for block in range(blocks):
                attend(level, block)

            @pl.loop(0, wide_n)
            def _(source):
                give_back(level, source)

    for_level(own_clusters)

    def wait_back(level, head, step):
        owner, there, offset = place(level, head, step)
        size = pads[level]

        @pl.when(there != me)
        def _():
            send(answers.at[pl.ds(0, size)], ret.at[head, pl.ds(offset, size)],
                 back_s.at[0], back_r.at[owner], wide=there).wait_recv()

    each_owner(wait_back)
    att2_sends = [share(att2, att2_sems, half) for half in range(2)]
    for half in range(2):
        rows = pl.ds(half * BLOCK, BLOCK)
        for h in range(heads):
            att2[n, rows, pl.ds(h * HEAD_DIM, HEAD_DIM)] = dot(to_token[h, rows, :], ret[h]).astype(BF16)
        att2_sends[half][0].start()
        att2_sends[half][1].start()
    for copy in w2_sends:
        copy.wait_recv()
    for half in range(2):
        att2_sends[half][0].wait_recv()
        att2_sends[half][2].start()
    for half in range(2):
        rows = pl.ds(half * BLOCK, BLOCK)
        att2_sends[half][1].wait_recv()
        att2_sends[half][2].wait_recv()
        total = hidden[rows, pl.ds(pl.multiple_of(n * cols, cols), cols)].astype(F32)
        for g in range(4):
            total = total + dot(att2[g, rows, :], w2[g])
        out[rows, :] = total

    for copy in (w1_far, w1_near, w1_swap, *w1_fwd, *w2_sends, *att1_sends[0], *att1_sends[1], *att2_sends[0], *att2_sends[1]):
        copy.wait_send()

    @pl.when(me < wide_n - 1)
    def _():
        halo.wait_send()

    def sent(level, head, step):
        there, copy, _ = go(level, head, step)

        @pl.when(there != me)
        def _():
            copy.wait_send()

    each_owner(sent)

    def sent_back(level):
        @pl.loop(0, wide_n)
        def _(source):
            @pl.when(source != me)
            def _():
                back_copy(level, source)[2].wait_send()

    for_level(sent_back)


def solution(mesh):
    wide_n = mesh.shape["wide"]

    def shards(tokens, w_qk1, w_value1, w_out1, w_qk2, w_value2, w_out2, cluster_ids):
        length, width = tokens.shape
        cols = w_qk1.shape[1]
        heads = cols // HEAD_DIM
        clusters = wide_n // heads
        cap = 2 * length * heads // wide_n
        sizes = (cap, 3 * cap // 8, cap // 4)
        pads = tuple(-(-size // 16) * 16 for size in sizes)
        slots = clusters // 4 * pads[0] + clusters // 2 * pads[1] + clusters // 4 * pads[2]
        most = wide_n * pads[0]
        groups = mesh.shape["narrow"]
        dma = pltpu.SemaphoreType.DMA
        vmem = pl.BlockSpec(memory_space=pltpu.VMEM)
        return pl.pallas_call(
            functools.partial(whole_kernel, wide_n, heads, clusters, sizes, pads, slots),
            out_shape=jax.ShapeDtypeStruct((length, cols), F32),
            in_specs=[vmem] * 8,
            out_specs=vmem,
            scratch_shapes=[
                pltpu.VMEM((WINDOW + length, 2 * cols), BF16),
                pltpu.VMEM((groups, cols, width), BF16),
                pltpu.VMEM((groups, length, cols), BF16),
                pltpu.VMEM((length, width), BF16),
                pltpu.VMEM((length, width), BF16),
                pltpu.VMEM((heads, slots, length), BF16),
                pltpu.VMEM((heads, length, slots), BF16),
                pltpu.VMEM((heads, slots, 2 * HEAD_DIM), BF16),
                pltpu.VMEM((most, 2 * HEAD_DIM), BF16),
                pltpu.VMEM((HEAD_DIM, most), BF16),
                pltpu.VMEM((most, HEAD_DIM), BF16),
                pltpu.VMEM((heads, slots, HEAD_DIM), BF16),
                pltpu.VMEM((groups, length, cols), BF16),
                pltpu.VMEM((groups, cols, cols), BF16),
                dma((2,)), dma((2, 5)), dma((2, 2, 3)), dma((2, 3)),
                dma((wide_n,)), dma((wide_n,)), dma((wide_n,)), dma((wide_n,)),
                dma((2, 2, 3)), dma,
            ],
            compiler_params=pltpu.CompilerParams(
                collective_id=0, has_side_effects=True, vmem_limit_bytes=56 * 1024 * 1024),
        )(tokens, w_qk1, w_value1, w_out1, w_qk2, w_value2, w_out2, cluster_ids)

    placed = (
        P("wide", None),
        P(None, "narrow"),
        P(None, "narrow"),
        P("narrow", None),
        P(None, "narrow"),
        P(None, "narrow"),
        P("narrow", None),
        P("narrow", "wide"),
    )
    return jax.shard_map(
        shards, mesh=mesh, in_specs=placed, out_specs=P("wide", "narrow"), check_vma=False
    )
```

```python
import functools
import math

import jax
import jax.numpy as jnp
from jax import lax
from jax.experimental import pallas as pl
from jax.experimental.pallas import tpu as pltpu
from jax.sharding import PartitionSpec as P

HEAD_DIM = 128
WINDOW = 256
EPS = 1e-06
BLOCK = 256
SCALE = math.log2(math.e) / math.sqrt(HEAD_DIM)
LOW = -1e30
MESH = pl.DeviceIdType.MESH
F32 = jnp.float32
BF16 = jnp.bfloat16


def flip(index, bit):
    return index + bit - 2 * bit * lax.rem(lax.div(index, bit), 2)


def rms_round(rows):
    values = rows.astype(F32)
    factor = lax.rsqrt(jnp.mean(values * values, axis=-1, keepdims=True) + EPS)
    return (values * factor).astype(BF16)


def dot(a, b):
    return jnp.dot(a, b, preferred_element_type=F32)


def dot_nt(a, b):
    return lax.dot_general(a, b, (((1,), (1,)), ((), ())), preferred_element_type=F32)


def dot_tn(a, b):
    return lax.dot_general(a, b, (((0,), (0,)), ((), ())), preferred_element_type=F32)


def send(src, dst, send_sem, recv_sem, **where):
    return pltpu.make_async_remote_copy(
        src_ref=src, dst_ref=dst, send_sem=send_sem, recv_sem=recv_sem,
        device_id=where, device_id_type=MESH)


def whole_kernel(wide_n, heads, clusters, sizes, pads, slots,
                 tokens_in, w_qk1, w_value1, w_out1, w_qk2, w_value2, w_out2, ids_in, out,
                 tokens, wkv1, wkv2, ids, kvx, w1, att1, hidden, normed2, to_slot, to_token, packed, arrived, value_t, answers, ret, att2, w2,
                 halo_sem, w1_sems, att1_sems, w2_sems, go_s, go_r, back_s, back_r, att2_sems, local_sem, load_sems):
    me, n = lax.axis_index("wide"), lax.axis_index("narrow")
    near, far = flip(n, 1), flip(n, 2)
    cross = flip(near, 2)
    length = tokens_in.shape[0]
    cols = w_qk1.shape[1]
    counts = (clusters // 4, clusters // 2, clusters // 4)
    starts = (0, clusters // 4, 3 * clusters // 4)
    bases = (0, counts[0] * pads[0], counts[0] * pads[0] + counts[1] * pads[1])
    core = lax.rem(n, 2)

    def shuffle(place):
        low = flip(place, 2)
        high = flip(place, 1)
        return jnp.where(place < wide_n // 2, low, high)

    def flip_core(place):
        return jnp.where(core == 1, flip(place, 1), place)

    def device_of(owner):
        return flip_core(shuffle(owner))

    mine = shuffle(flip_core(me))
    my_head, my_rank = lax.div(mine, clusters), lax.rem(mine, clusters)

    barrier = pltpu.get_barrier_semaphore()

    @pl.loop(1, wide_n)
    def _(k):
        pl.semaphore_signal(barrier, inc=1, device_id={"wide": lax.rem(me + k, wide_n)}, device_id_type=MESH)

    for other in (near, far, cross):
        pl.semaphore_signal(barrier, inc=1, device_id={"narrow": other}, device_id_type=MESH)

    mine_cols = pl.ds(pl.multiple_of(n * cols, cols), cols)
    loads = [(tokens_in, tokens), (w_qk1, wkv1.at[:, pl.ds(0, cols)]), (w_value1, wkv1.at[:, pl.ds(cols, cols)]),
             (ids_in, ids), (w_out1, w1.at[n]), (w_out2.at[:, mine_cols], w2.at[n])]
    for h in range(heads):
        part = pl.ds(h * HEAD_DIM, HEAD_DIM)
        loads.append((w_qk2.at[:, part], wkv2.at[h, :, pl.ds(0, HEAD_DIM)]))
        loads.append((w_value2.at[:, part], wkv2.at[h, :, pl.ds(HEAD_DIM, HEAD_DIM)]))
    loads = [pltpu.make_async_copy(src, dst, load_sems.at[index]) for index, (src, dst) in enumerate(loads)]
    for copy in loads:
        copy.start()

    def project1(start):
        rows = pl.ds(start, BLOCK)
        normed = rms_round(tokens[rows, :])
        there = pl.ds(WINDOW + start, BLOCK)
        kvx[there, :] = dot(normed, wkv1[...]).astype(BF16)

    tail = length - BLOCK
    quarter = cols // 4
    beside = flip(me, 2)
    parity = lax.rem(lax.div(me, 2), 2)
    early = [pl.ds(pl.multiple_of((2 * parity + c) * quarter, quarter), quarter) for c in range(2)]
    late = [pl.ds(pl.multiple_of((2 - 2 * parity + c) * quarter, quarter), quarter) for c in range(2)]
    w1_far = [send(w_out1.at[early[c]], w1.at[n, early[c]], w1_sems.at[0, c], w1_sems.at[1, c], narrow=far)
              for c in range(2)]
    w1_near = send(w_out1, w1.at[n], w1_sems.at[0, 2], w1_sems.at[1, 2], narrow=near)
    w1_swap = [send(w1.at[far, early[c]], w1.at[far, early[c]], w1_sems.at[0, 3 + c], w1_sems.at[1, 3 + c],
                    wide=beside) for c in range(2)]
    w1_fwd = [send(w1.at[far, rows], w1.at[far, rows], w1_sems.at[0, 5 + c], w1_sems.at[1, 5 + c], narrow=near)
              for c, rows in enumerate(early + late)]
    halo = send(kvx.at[pl.ds(length, WINDOW)], kvx.at[pl.ds(0, WINDOW)], halo_sem.at[0], halo_sem.at[1],
                wide=lax.rem(me + 1, wide_n))
    pl.semaphore_wait(barrier, wide_n - 1 + 3)
    for copy in w1_far:
        copy.start()
    for copy in loads[:3]:
        copy.wait()
    project1(tail)

    @pl.when(me < wide_n - 1)
    def _():
        halo.start()

    w1_near.start()

    @pl.when(me == 0)
    def _():
        kvx[pl.ds(0, WINDOW), :] = jnp.zeros((WINDOW, 2 * cols), BF16)

    project1(0)

    def window(start):
        key_at = lax.broadcasted_iota(jnp.int32, (2 * BLOCK, BLOCK), 0) + (me * length + start - WINDOW)
        query_at = lax.broadcasted_iota(jnp.int32, (2 * BLOCK, BLOCK), 1) + (me * length + start)
        gap = query_at - key_at
        keep = (gap > 0) & (gap < WINDOW) & (key_at >= 0) | (gap == 0) & (query_at == 0)
        for h in range(heads):
            q = kvx[pl.ds(start + WINDOW, BLOCK), pl.ds(h * HEAD_DIM, HEAD_DIM)]
            k = kvx[pl.ds(start, 2 * BLOCK), pl.ds(h * HEAD_DIM, HEAD_DIM)]
            v = kvx[pl.ds(start, 2 * BLOCK), pl.ds(cols + h * HEAD_DIM, HEAD_DIM)]
            scores = jnp.where(keep, dot_nt(k, q) * SCALE, LOW)
            top = jnp.max(scores, axis=0, keepdims=True)
            weights = jnp.exp2(scores - top)
            total = jnp.sum(weights, axis=0, keepdims=True)
            mixed = dot_tn(v, weights.astype(BF16)) / total
            att1[n, pl.ds(start, BLOCK), pl.ds(h * HEAD_DIM, HEAD_DIM)] = mixed.T.astype(BF16)

    def share(buffer, sems, half, size):
        rows = pl.ds(half * size, size)
        first = send(buffer.at[n, rows], buffer.at[n, rows], sems.at[0, half, 0], sems.at[1, half, 0], narrow=far)
        second = send(buffer.at[n, rows], buffer.at[n, rows], sems.at[0, half, 1], sems.at[1, half, 1], narrow=near)
        third = send(buffer.at[far, rows], buffer.at[far, rows], sems.at[0, half, 2], sems.at[1, half, 2],
                     narrow=near)
        return first, second, third

    att1_sends = [share(att1, att1_sems, half, BLOCK) for half in range(2)]
    window(tail)
    att1_sends[1][0].start()
    att1_sends[1][1].start()
    most = 128
    before = (lax.broadcasted_iota(jnp.int32, (length, length), 0)
              <= lax.broadcasted_iota(jnp.int32, (length, length), 1)).astype(F32).astype(BF16)

    def slot_of(h):
        match = (lax.broadcasted_iota(jnp.int32, (most, length), 0) == ids[pl.ds(h, 1), :]).astype(F32)
        match16 = match.astype(BF16)
        running = dot(match16, before)
        held = jnp.sum(match, axis=1, keepdims=True)
        held_row = dot_nt(jnp.ones((8, length), BF16), match16)[0:1, :]
        lower = (lax.broadcasted_iota(jnp.int32, (most, most), 1)
                 < lax.broadcasted_iota(jnp.int32, (most, most), 0))
        ahead = (held_row > held) | (held_row == held) & lower
        rank = jnp.sum(ahead.astype(F32), axis=1, keepdims=True)
        base = jnp.where(
            rank < starts[1], rank * pads[0],
            jnp.where(rank < starts[2], bases[1] + (rank - starts[1]) * pads[1],
                      bases[2] + (rank - starts[2]) * pads[2]))
        target = jnp.sum(match * (base + running - 1.0), axis=0, keepdims=True)
        target_col = jnp.broadcast_to(target, (8, length)).T[:, 0:1].astype(jnp.int32)
        target = target.astype(jnp.int32)
        to_slot[h] = (lax.broadcasted_iota(jnp.int32, (slots, length), 0) == target).astype(F32).astype(BF16)
        to_token[h] = (lax.broadcasted_iota(jnp.int32, (length, slots), 1) == target_col).astype(F32).astype(BF16)

    loads[3].wait()
    for c in range(2):
        w1_far[c].wait_recv()
        w1_swap[c].start()
        w1_fwd[c].start()
        if c < heads:
            slot_of(c)
    for h in range(2, heads):
        slot_of(h)

    @pl.when(me > 0)
    def _():
        halo.wait_recv()

    window(0)
    att1_sends[0][0].start()
    att1_sends[0][1].start()

    att1_sends[1][0].wait_recv()
    att1_sends[1][2].start()
    w1_swap[0].wait_recv()
    w1_fwd[2].start()
    att1_sends[0][0].wait_recv()
    att1_sends[0][2].start()
    w1_swap[1].wait_recv()
    w1_fwd[3].start()
    for copy in loads[4:]:
        copy.wait()
    w1_near.wait_recv()
    for copy in w1_fwd:
        copy.wait_recv()

    for half in (1, 0):
        first, second, third = att1_sends[half]
        second.wait_recv()
        third.wait_recv()
        rows = pl.ds(half * BLOCK, BLOCK)
        total = tokens[rows, :].astype(F32)
        for g in range(4):
            total = total + dot(att1[g, rows, :], w1[g])
        hidden16 = total.astype(BF16)
        hidden[rows, :] = hidden16
        normed2[rows, :] = rms_round(hidden16)

    def place(level, head, step):
        rank = starts[level] + step
        owner = head * clusters + rank
        offset = pl.multiple_of(bases[level] + step * pads[level], 16)
        return owner, device_of(owner), offset

    def go(level, head, step):
        owner, there, offset = place(level, head, step)
        size = pads[level]
        return there, send(packed.at[head, pl.ds(offset, size)],
                           arrived.at[pl.ds(pl.multiple_of(me * size, 16), size)],
                           go_s.at[owner], go_r.at[me], wide=there), (head, offset, size)

    def each_owner(body):
        for level in range(3):
            @pl.loop(0, heads * counts[level])
            def _(item):
                body(level, lax.div(item, counts[level]), lax.rem(item, counts[level]))

    def start_go(level, head, step):
        there, copy, (_, offset, size) = go(level, head, step)

        @pl.when(there != me)
        def _():
            copy.start()

        @pl.when(there == me)
        def _():
            own = pltpu.make_async_copy(packed.at[head, pl.ds(offset, size)],
                                        arrived.at[pl.ds(pl.multiple_of(me * size, 16), size)], local_sem)
            own.start()
            own.wait()

    for h in range(heads):
        packed[h] = dot(to_slot[h], dot(normed2[...], wkv2[h]).astype(BF16)).astype(BF16)
        for level in range(3):
            @pl.loop(0, counts[level])
            def _(step):
                start_go(level, h, step)

    w2_sends = []
    for index, other in enumerate((near, far, cross)):
        w2_sends.append(send(w_out2.at[:, pl.ds(pl.multiple_of(other * cols, cols), cols)], w2.at[n],
                             w2_sems.at[0, index], w2_sems.at[1, index], narrow=other))
        w2_sends[-1].start()

    def for_level(body):
        for level in range(3):
            @pl.when((my_rank >= starts[level]) & (my_rank < starts[level] + counts[level]))
            def _():
                body(level)

    def from_source(level, source):
        size = pads[level]
        rows = pl.ds(pl.multiple_of(source * size, 16), size)
        return send(packed.at[0, pl.ds(0, size)], arrived.at[rows], go_s.at[0], go_r.at[source], wide=source)

    def back_copy(level, source):
        size = pads[level]
        rows = pl.ds(pl.multiple_of(source * size, 16), size)
        offset = pl.multiple_of(bases[level] + (my_rank - starts[level]) * size, 16)
        return rows, offset, send(answers.at[rows], ret.at[my_head, pl.ds(offset, size)],
                                  back_s.at[source], back_r.at[mine], wide=source)

    def receive(level, source):
        @pl.when(source != me)
        def _():
            from_source(level, source).wait_recv()

    def give_back(level, source):
        rows, offset, copy = back_copy(level, source)

        @pl.when(source != me)
        def _():
            copy.start()

        @pl.when(source == me)
        def _():
            own = pltpu.make_async_copy(answers.at[rows], ret.at[my_head, pl.ds(offset, pads[level])], local_sem)
            own.start()
            own.wait()

    def attend(level, block):
        size, real = pads[level], sizes[level]
        begin = block * BLOCK
        here = pl.ds(begin, BLOCK)
        q = arrived[here, pl.ds(0, HEAD_DIM)]
        value_t[:, here] = arrived[here, pl.ds(HEAD_DIM, HEAD_DIM)].T

        def score(first, rows, diagonal):
            scores = dot_nt(arrived[pl.ds(first, rows), pl.ds(0, HEAD_DIM)], q) * SCALE
            keep = None
            key_at = lax.broadcasted_iota(jnp.int32, (rows, BLOCK), 0)
            if diagonal:
                query_at = lax.broadcasted_iota(jnp.int32, (rows, BLOCK), 1)
                keep = key_at < query_at
                if block == 0:
                    keep = keep | (key_at + query_at == 0)
            if size != real:
                live = lax.rem(key_at + first, size) < real
                keep = live if keep is None else keep & live
            return scores if keep is None else jnp.where(keep, scores, LOW)

        parts = [(begin, score(begin, BLOCK, True))]
        if block > 0:
            parts.append((0, score(0, begin, False)))
        top = functools.reduce(jnp.maximum, [jnp.max(scores, axis=0, keepdims=True) for _, scores in parts])
        total, mixed = 0.0, 0.0
        for first, scores in parts:
            weights = jnp.exp2(scores - top)
            total = total + jnp.sum(weights, axis=0, keepdims=True)
            mixed = mixed + dot(value_t[:, pl.ds(first, scores.shape[0])], weights.astype(BF16))
        answers[here, :] = (mixed / total).T.astype(BF16)

    def own_clusters(level):
        size = pads[level]
        came, gone = 0, 0
        for block in range(wide_n * size // BLOCK):
            end = (block + 1) * BLOCK

            @pl.loop(came, -(-end // size))
            def _(source):
                receive(level, source)

            attend(level, block)

            @pl.loop(gone, end // size)
            def _(source):
                give_back(level, source)

            came, gone = -(-end // size), end // size

    for_level(own_clusters)

    def wait_back(level, head, step):
        owner, there, offset = place(level, head, step)
        size = pads[level]

        @pl.when(there != me)
        def _():
            send(answers.at[pl.ds(0, size)], ret.at[head, pl.ds(offset, size)],
                 back_s.at[0], back_r.at[owner], wide=there).wait_recv()

    each_owner(wait_back)
    pieces, piece = 4, length // 4
    att2_sends = [share(att2, att2_sems, part, piece) for part in range(pieces)]
    for part in range(pieces):
        rows = pl.ds(part * piece, piece)
        for h in range(heads):
            att2[n, rows, pl.ds(h * HEAD_DIM, HEAD_DIM)] = dot(to_token[h, rows, :], ret[h]).astype(BF16)
        att2_sends[part][0].start()
        att2_sends[part][1].start()
    for copy in w2_sends:
        copy.wait_recv()

    def result(part):
        rows = pl.ds(part * piece, piece)
        att2_sends[part][1].wait_recv()
        att2_sends[part][2].wait_recv()
        total = hidden[rows, mine_cols].astype(F32)
        for g in range(4):
            total = total + dot(att2[g, rows, :], w2[g])
        out[rows, :] = total

    for part in range(pieces):
        att2_sends[part][0].wait_recv()
        att2_sends[part][2].start()
        if part > 0:
            result(part - 1)
    result(pieces - 1)

    for copy in (*w1_far, w1_near, *w1_swap, *w1_fwd, *w2_sends,
                 *(copy for copies in att1_sends + att2_sends for copy in copies)):
        copy.wait_send()

    @pl.when(me < wide_n - 1)
    def _():
        halo.wait_send()

    def sent(level, head, step):
        there, copy, _ = go(level, head, step)

        @pl.when(there != me)
        def _():
            copy.wait_send()

    each_owner(sent)

    def sent_back(level):
        @pl.loop(0, wide_n)
        def _(source):
            @pl.when(source != me)
            def _():
                back_copy(level, source)[2].wait_send()

    for_level(sent_back)


def solution(mesh):
    wide_n = mesh.shape["wide"]

    def shards(tokens, w_qk1, w_value1, w_out1, w_qk2, w_value2, w_out2, cluster_ids):
        length, width = tokens.shape
        cols = w_qk1.shape[1]
        heads = cols // HEAD_DIM
        clusters = wide_n // heads
        cap = 2 * length * heads // wide_n
        sizes = (cap, 3 * cap // 8, cap // 4)
        pads = tuple(-(-size // 16) * 16 for size in sizes)
        slots = clusters // 4 * pads[0] + clusters // 2 * pads[1] + clusters // 4 * pads[2]
        most = wide_n * pads[0]
        groups = mesh.shape["narrow"]
        dma = pltpu.SemaphoreType.DMA
        vmem = pl.BlockSpec(memory_space=pltpu.VMEM)
        return pl.pallas_call(
            functools.partial(whole_kernel, wide_n, heads, clusters, sizes, pads, slots),
            out_shape=jax.ShapeDtypeStruct((length, cols), F32),
            in_specs=[pl.BlockSpec(memory_space=pl.ANY)] * 8,
            out_specs=vmem,
            scratch_shapes=[
                pltpu.VMEM((length, width), BF16),
                pltpu.VMEM((width, 2 * cols), BF16),
                pltpu.VMEM((heads, width, 2 * HEAD_DIM), BF16),
                pltpu.VMEM((heads, length), jnp.int32),
                pltpu.VMEM((WINDOW + length, 2 * cols), BF16),
                pltpu.VMEM((groups, cols, width), BF16),
                pltpu.VMEM((groups, length, cols), BF16),
                pltpu.VMEM((length, width), BF16),
                pltpu.VMEM((length, width), BF16),
                pltpu.VMEM((heads, slots, length), BF16),
                pltpu.VMEM((heads, length, slots), BF16),
                pltpu.VMEM((heads, slots, 2 * HEAD_DIM), BF16),
                pltpu.VMEM((most, 2 * HEAD_DIM), BF16),
                pltpu.VMEM((HEAD_DIM, most), BF16),
                pltpu.VMEM((most, HEAD_DIM), BF16),
                pltpu.VMEM((heads, slots, HEAD_DIM), BF16),
                pltpu.VMEM((groups, length, cols), BF16),
                pltpu.VMEM((groups, cols, cols), BF16),
                dma((2,)), dma((2, 9)), dma((2, 2, 3)), dma((2, 3)),
                dma((wide_n,)), dma((wide_n,)), dma((wide_n,)), dma((wide_n,)),
                dma((2, 4, 3)), dma, dma((6 + 2 * heads,)),
            ],
            compiler_params=pltpu.CompilerParams(
                collective_id=0, has_side_effects=True, vmem_limit_bytes=56 * 1024 * 1024),
        )(tokens, w_qk1, w_value1, w_out1, w_qk2, w_value2, w_out2, cluster_ids)

    placed = (
        P("wide", None),
        P(None, "narrow"),
        P(None, "narrow"),
        P("narrow", None),
        P(None, "narrow"),
        P(None, "narrow"),
        P("narrow", None),
        P("narrow", "wide"),
    )
    return jax.shard_map(
        shards, mesh=mesh, in_specs=placed, out_specs=P("wide", "narrow"), check_vma=False
    )
```

```python
import functools
import math

import jax
import jax.numpy as jnp
from jax import lax
from jax.experimental import pallas as pl
from jax.experimental.pallas import tpu as pltpu
from jax.sharding import PartitionSpec as P

HEAD_DIM = 128
WINDOW = 256
EPS = 1e-06
BLOCK = 256
PIECE = 128
SCALE = math.log2(math.e) / math.sqrt(HEAD_DIM)
LOW = -1e30
MESH = pl.DeviceIdType.MESH
F32 = jnp.float32
BF16 = jnp.bfloat16


def flip(index, bit):
    return index + bit - 2 * bit * lax.rem(lax.div(index, bit), 2)


def rms_round(rows):
    values = rows.astype(F32)
    factor = lax.rsqrt(jnp.mean(values * values, axis=-1, keepdims=True) + EPS)
    return (values * factor).astype(BF16)


def dot(a, b):
    return jnp.dot(a, b, preferred_element_type=F32)


def dot_nt(a, b):
    return lax.dot_general(a, b, (((1,), (1,)), ((), ())), preferred_element_type=F32)


def dot_tn(a, b):
    return lax.dot_general(a, b, (((0,), (0,)), ((), ())), preferred_element_type=F32)


def send(src, dst, send_sem, recv_sem, **where):
    return pltpu.make_async_remote_copy(
        src_ref=src, dst_ref=dst, send_sem=send_sem, recv_sem=recv_sem,
        device_id=where, device_id_type=MESH)


def whole_kernel(wide_n, heads, clusters, sizes, pads, slots,
                 tokens_in, w_qk1, w_value1, w_out1, w_qk2, w_value2, w_out2, ids_in, out,
                 tokens, wkv1, wkv2, ids, kvx, w1, att1, hidden, normed2, to_slot, to_token, packed, arrived, value_t, answers, ret, att2, w2,
                 halo_sem, w1_sems, att1_sems, w2_sems, go_s, go_r, back_s, back_r, att2_sems, local_sem, load_sems):
    me, n = lax.axis_index("wide"), lax.axis_index("narrow")
    near, far = flip(n, 1), flip(n, 2)
    cross = flip(near, 2)
    length = tokens_in.shape[0]
    cols = w_qk1.shape[1]
    counts = (clusters // 4, clusters // 2, clusters // 4)
    starts = (0, clusters // 4, 3 * clusters // 4)
    bases = (0, counts[0] * pads[0], counts[0] * pads[0] + counts[1] * pads[1])
    core = lax.rem(n, 2)

    def shuffle(place):
        low = flip(place, 2)
        high = flip(place, 1)
        return jnp.where(place < wide_n // 2, low, high)

    def flip_core(place):
        return jnp.where(core == 1, flip(place, 1), place)

    def device_of(owner):
        return flip_core(shuffle(owner))

    mine = shuffle(flip_core(me))
    my_head, my_rank = lax.div(mine, clusters), lax.rem(mine, clusters)

    barrier = pltpu.get_barrier_semaphore()

    @pl.loop(1, wide_n)
    def _(k):
        pl.semaphore_signal(barrier, inc=1, device_id={"wide": lax.rem(me + k, wide_n)}, device_id_type=MESH)

    for other in (near, far, cross):
        pl.semaphore_signal(barrier, inc=1, device_id={"narrow": other}, device_id_type=MESH)

    mine_cols = pl.ds(pl.multiple_of(n * cols, cols), cols)
    loads = [(tokens_in, tokens), (w_qk1, wkv1.at[:, pl.ds(0, cols)]), (w_value1, wkv1.at[:, pl.ds(cols, cols)]),
             (ids_in, ids), (w_out1, w1.at[n]), (w_out2.at[:, mine_cols], w2.at[n])]
    for h in range(heads):
        part = pl.ds(h * HEAD_DIM, HEAD_DIM)
        loads.append((w_qk2.at[:, part], wkv2.at[h, :, pl.ds(0, HEAD_DIM)]))
        loads.append((w_value2.at[:, part], wkv2.at[h, :, pl.ds(HEAD_DIM, HEAD_DIM)]))
    loads = [pltpu.make_async_copy(src, dst, load_sems.at[index]) for index, (src, dst) in enumerate(loads)]
    for copy in loads:
        copy.start()

    def project1(start):
        rows = pl.ds(start, BLOCK)
        normed = rms_round(tokens[rows, :])
        there = pl.ds(WINDOW + start, BLOCK)
        kvx[there, :] = dot(normed, wkv1[...]).astype(BF16)

    tail = length - BLOCK
    quarter = cols // 4
    beside = flip(me, 2)
    parity = lax.rem(lax.div(me, 2), 2)
    early = [pl.ds(pl.multiple_of((2 * parity + c) * quarter, quarter), quarter) for c in range(2)]
    late = [pl.ds(pl.multiple_of((2 - 2 * parity + c) * quarter, quarter), quarter) for c in range(2)]
    w1_far = [send(w_out1.at[early[c]], w1.at[n, early[c]], w1_sems.at[0, c], w1_sems.at[1, c], narrow=far)
              for c in range(2)]
    w1_near = send(w_out1, w1.at[n], w1_sems.at[0, 2], w1_sems.at[1, 2], narrow=near)
    w1_swap = [send(w1.at[far, early[c]], w1.at[far, early[c]], w1_sems.at[0, 3 + c], w1_sems.at[1, 3 + c],
                    wide=beside) for c in range(2)]
    w1_fwd = [send(w1.at[far, rows], w1.at[far, rows], w1_sems.at[0, 5 + c], w1_sems.at[1, 5 + c], narrow=near)
              for c, rows in enumerate(early + late)]
    halo = [send(kvx.at[pl.ds(length + start, PIECE)], kvx.at[pl.ds(start, PIECE)], halo_sem.at[0, c],
                 halo_sem.at[1, c], wide=lax.rem(me + 1, wide_n)) for c, start in enumerate((PIECE, 0))]
    pl.semaphore_wait(barrier, wide_n - 1 + 3)
    for copy in w1_far:
        copy.start()
    for copy in loads[:3]:
        copy.wait()
    project1(tail)

    @pl.when(me < wide_n - 1)
    def _():
        for copy in halo:
            copy.start()

    w1_near.start()

    @pl.when(me == 0)
    def _():
        kvx[pl.ds(0, WINDOW), :] = jnp.zeros((WINDOW, 2 * cols), BF16)

    project1(0)

    def window(start):
        key_at = lax.broadcasted_iota(jnp.int32, (WINDOW + PIECE, PIECE), 0) + (me * length + start - WINDOW)
        query_at = lax.broadcasted_iota(jnp.int32, (WINDOW + PIECE, PIECE), 1) + (me * length + start)
        gap = query_at - key_at
        keep = (gap > 0) & (gap < WINDOW) & (key_at >= 0) | (gap == 0) & (query_at == 0)
        for h in range(heads):
            q = kvx[pl.ds(start + WINDOW, PIECE), pl.ds(h * HEAD_DIM, HEAD_DIM)]
            k = kvx[pl.ds(start, WINDOW + PIECE), pl.ds(h * HEAD_DIM, HEAD_DIM)]
            v = kvx[pl.ds(start, WINDOW + PIECE), pl.ds(cols + h * HEAD_DIM, HEAD_DIM)]
            scores = jnp.where(keep, dot_nt(k, q) * SCALE, LOW)
            top = jnp.max(scores, axis=0, keepdims=True)
            weights = jnp.exp2(scores - top)
            total = jnp.sum(weights, axis=0, keepdims=True)
            mixed = dot_tn(v, weights.astype(BF16)) / total
            att1[n, pl.ds(start, PIECE), pl.ds(h * HEAD_DIM, HEAD_DIM)] = mixed.T.astype(BF16)

    def share(buffer, sems, half, size):
        rows = pl.ds(half * size, size)
        first = send(buffer.at[n, rows], buffer.at[n, rows], sems.at[0, half, 0], sems.at[1, half, 0], narrow=far)
        second = send(buffer.at[n, rows], buffer.at[n, rows], sems.at[0, half, 1], sems.at[1, half, 1], narrow=near)
        third = send(buffer.at[far, rows], buffer.at[far, rows], sems.at[0, half, 2], sems.at[1, half, 2],
                     narrow=near)
        return first, second, third

    att1_sends = [share(att1, att1_sems, part, PIECE) for part in range(4)]
    def attend_window(part):
        window(part * PIECE)
        att1_sends[part][0].start()
        att1_sends[part][1].start()

    attend_window(3)
    attend_window(2)
    most = 128
    before = (lax.broadcasted_iota(jnp.int32, (length, length), 0)
              <= lax.broadcasted_iota(jnp.int32, (length, length), 1)).astype(F32).astype(BF16)

    def slot_of(h):
        match = (lax.broadcasted_iota(jnp.int32, (most, length), 0) == ids[pl.ds(h, 1), :]).astype(F32)
        match16 = match.astype(BF16)
        running = dot(match16, before)
        held = jnp.sum(match, axis=1, keepdims=True)
        held_row = dot_nt(jnp.ones((8, length), BF16), match16)[0:1, :]
        lower = (lax.broadcasted_iota(jnp.int32, (most, most), 1)
                 < lax.broadcasted_iota(jnp.int32, (most, most), 0))
        ahead = (held_row > held) | (held_row == held) & lower
        rank = jnp.sum(ahead.astype(F32), axis=1, keepdims=True)
        base = jnp.where(
            rank < starts[1], rank * pads[0],
            jnp.where(rank < starts[2], bases[1] + (rank - starts[1]) * pads[1],
                      bases[2] + (rank - starts[2]) * pads[2]))
        target = jnp.sum(match * (base + running - 1.0), axis=0, keepdims=True)
        target_col = jnp.broadcast_to(target, (8, length)).T[:, 0:1].astype(jnp.int32)
        target = target.astype(jnp.int32)
        to_slot[h] = (lax.broadcasted_iota(jnp.int32, (slots, length), 0) == target).astype(F32).astype(BF16)
        to_token[h] = (lax.broadcasted_iota(jnp.int32, (length, slots), 1) == target_col).astype(F32).astype(BF16)

    loads[3].wait()
    for c in range(2):
        w1_far[c].wait_recv()
        w1_swap[c].start()
        w1_fwd[c].start()
        if c < heads:
            slot_of(c)
    for h in range(2, heads):
        slot_of(h)

    for part in (1, 0):
        @pl.when(me > 0)
        def _():
            halo[1 - part].wait_recv()

        attend_window(part)

    def forward(part):
        att1_sends[part][0].wait_recv()
        att1_sends[part][2].start()

    forward(3)
    forward(2)
    w1_swap[0].wait_recv()
    w1_fwd[2].start()
    forward(1)
    w1_swap[1].wait_recv()
    w1_fwd[3].start()
    for copy in loads[4:]:
        copy.wait()
    w1_near.wait_recv()
    for copy in w1_fwd:
        copy.wait_recv()

    def rest(parts):
        for part in parts:
            att1_sends[part][1].wait_recv()
            att1_sends[part][2].wait_recv()
        rows = pl.ds(parts[-1] * PIECE, len(parts) * PIECE)
        total = tokens[rows, :].astype(F32)
        for g in range(4):
            total = total + dot(att1[g, rows, :], w1[g])
        hidden16 = total.astype(BF16)
        hidden[rows, :] = hidden16
        normed2[rows, :] = rms_round(hidden16)

    rest((3, 2))
    forward(0)
    rest((1, 0))

    def place(level, head, step):
        rank = starts[level] + step
        owner = head * clusters + rank
        offset = pl.multiple_of(bases[level] + step * pads[level], 16)
        return owner, device_of(owner), offset

    def go(level, head, step):
        owner, there, offset = place(level, head, step)
        size = pads[level]
        return there, send(packed.at[head, pl.ds(offset, size)],
                           arrived.at[pl.ds(pl.multiple_of(me * size, 16), size)],
                           go_s.at[owner], go_r.at[me], wide=there), (head, offset, size)

    def each_owner(body):
        for level in range(3):
            @pl.loop(0, heads * counts[level])
            def _(item):
                body(level, lax.div(item, counts[level]), lax.rem(item, counts[level]))

    def start_go(level, head, step):
        there, copy, (_, offset, size) = go(level, head, step)

        @pl.when(there != me)
        def _():
            copy.start()

        @pl.when(there == me)
        def _():
            own = pltpu.make_async_copy(packed.at[head, pl.ds(offset, size)],
                                        arrived.at[pl.ds(pl.multiple_of(me * size, 16), size)], local_sem)
            own.start()
            own.wait()

    def leave(level, head):
        @pl.loop(0, counts[level])
        def _(step):
            start_go(level, head, step)

    for h in range(heads):
        packed[h] = dot(to_slot[h], dot(normed2[...], wkv2[h]).astype(BF16)).astype(BF16)
        leave(0, h)
    for level in (1, 2):
        for h in range(heads):
            leave(level, h)

    w2_sends = []
    for index, other in enumerate((near, far, cross)):
        w2_sends.append(send(w_out2.at[:, pl.ds(pl.multiple_of(other * cols, cols), cols)], w2.at[n],
                             w2_sems.at[0, index], w2_sems.at[1, index], narrow=other))
        w2_sends[-1].start()

    def for_level(body):
        for level in range(3):
            @pl.when((my_rank >= starts[level]) & (my_rank < starts[level] + counts[level]))
            def _():
                body(level)

    def from_source(level, source):
        size = pads[level]
        rows = pl.ds(pl.multiple_of(source * size, 16), size)
        return send(packed.at[0, pl.ds(0, size)], arrived.at[rows], go_s.at[0], go_r.at[source], wide=source)

    def back_copy(level, source):
        size = pads[level]
        rows = pl.ds(pl.multiple_of(source * size, 16), size)
        offset = pl.multiple_of(bases[level] + (my_rank - starts[level]) * size, 16)
        return rows, offset, send(answers.at[rows], ret.at[my_head, pl.ds(offset, size)],
                                  back_s.at[source], back_r.at[mine], wide=source)

    def receive(level, source):
        @pl.when(source != me)
        def _():
            from_source(level, source).wait_recv()

    def give_back(level, source):
        rows, offset, copy = back_copy(level, source)

        @pl.when(source != me)
        def _():
            copy.start()

        @pl.when(source == me)
        def _():
            own = pltpu.make_async_copy(answers.at[rows], ret.at[my_head, pl.ds(offset, pads[level])], local_sem)
            own.start()
            own.wait()

    def attend(level, block):
        size, real = pads[level], sizes[level]
        begin = block * BLOCK
        here = pl.ds(begin, BLOCK)
        q = arrived[here, pl.ds(0, HEAD_DIM)]
        value_t[:, here] = arrived[here, pl.ds(HEAD_DIM, HEAD_DIM)].T

        def score(first, rows, diagonal):
            scores = dot_nt(arrived[pl.ds(first, rows), pl.ds(0, HEAD_DIM)], q) * SCALE
            keep = None
            key_at = lax.broadcasted_iota(jnp.int32, (rows, BLOCK), 0)
            if diagonal:
                query_at = lax.broadcasted_iota(jnp.int32, (rows, BLOCK), 1)
                keep = key_at < query_at
                if block == 0:
                    keep = keep | (key_at + query_at == 0)
            if size != real:
                live = lax.rem(key_at + first, size) < real
                keep = live if keep is None else keep & live
            return scores if keep is None else jnp.where(keep, scores, LOW)

        parts = [(begin, score(begin, BLOCK, True))]
        if block > 0:
            parts.append((0, score(0, begin, False)))
        top = functools.reduce(jnp.maximum, [jnp.max(scores, axis=0, keepdims=True) for _, scores in parts])
        total, mixed = 0.0, 0.0
        for first, scores in parts:
            weights = jnp.exp2(scores - top)
            total = total + jnp.sum(weights, axis=0, keepdims=True)
            mixed = mixed + dot(value_t[:, pl.ds(first, scores.shape[0])], weights.astype(BF16))
        answers[here, :] = (mixed / total).T.astype(BF16)

    def own_clusters(level):
        size = pads[level]
        came, gone = 0, 0
        for block in range(wide_n * size // BLOCK):
            end = (block + 1) * BLOCK

            @pl.loop(came, -(-end // size))
            def _(source):
                receive(level, source)

            attend(level, block)

            @pl.loop(gone, end // size)
            def _(source):
                give_back(level, source)

            came, gone = -(-end // size), end // size

    for_level(own_clusters)

    def wait_back(level, head, step):
        owner, there, offset = place(level, head, step)
        size = pads[level]

        @pl.when(there != me)
        def _():
            send(answers.at[pl.ds(0, size)], ret.at[head, pl.ds(offset, size)],
                 back_s.at[0], back_r.at[owner], wide=there).wait_recv()

    each_owner(wait_back)
    pieces, piece = 4, length // 4
    att2_sends = [share(att2, att2_sems, part, piece) for part in range(pieces)]
    for part in range(pieces):
        rows = pl.ds(part * piece, piece)
        for h in range(heads):
            att2[n, rows, pl.ds(h * HEAD_DIM, HEAD_DIM)] = dot(to_token[h, rows, :], ret[h]).astype(BF16)
        att2_sends[part][0].start()
        att2_sends[part][1].start()
    for copy in w2_sends:
        copy.wait_recv()

    def result(part):
        rows = pl.ds(part * piece, piece)
        att2_sends[part][1].wait_recv()
        att2_sends[part][2].wait_recv()
        total = hidden[rows, mine_cols].astype(F32)
        for g in range(4):
            total = total + dot(att2[g, rows, :], w2[g])
        out[rows, :] = total

    for part in range(pieces):
        att2_sends[part][0].wait_recv()
        att2_sends[part][2].start()
        if part > 0:
            result(part - 1)
    result(pieces - 1)

    for copy in (*w1_far, w1_near, *w1_swap, *w1_fwd, *w2_sends,
                 *(copy for copies in att1_sends + att2_sends for copy in copies)):
        copy.wait_send()

    @pl.when(me < wide_n - 1)
    def _():
        for copy in halo:
            copy.wait_send()

    def sent(level, head, step):
        there, copy, _ = go(level, head, step)

        @pl.when(there != me)
        def _():
            copy.wait_send()

    each_owner(sent)

    def sent_back(level):
        @pl.loop(0, wide_n)
        def _(source):
            @pl.when(source != me)
            def _():
                back_copy(level, source)[2].wait_send()

    for_level(sent_back)


def solution(mesh):
    wide_n = mesh.shape["wide"]

    def shards(tokens, w_qk1, w_value1, w_out1, w_qk2, w_value2, w_out2, cluster_ids):
        length, width = tokens.shape
        cols = w_qk1.shape[1]
        heads = cols // HEAD_DIM
        clusters = wide_n // heads
        cap = 2 * length * heads // wide_n
        sizes = (cap, 3 * cap // 8, cap // 4)
        pads = tuple(-(-size // 16) * 16 for size in sizes)
        slots = clusters // 4 * pads[0] + clusters // 2 * pads[1] + clusters // 4 * pads[2]
        most = wide_n * pads[0]
        groups = mesh.shape["narrow"]
        dma = pltpu.SemaphoreType.DMA
        vmem = pl.BlockSpec(memory_space=pltpu.VMEM)
        return pl.pallas_call(
            functools.partial(whole_kernel, wide_n, heads, clusters, sizes, pads, slots),
            out_shape=jax.ShapeDtypeStruct((length, cols), F32),
            in_specs=[pl.BlockSpec(memory_space=pl.ANY)] * 8,
            out_specs=vmem,
            scratch_shapes=[
                pltpu.VMEM((length, width), BF16),
                pltpu.VMEM((width, 2 * cols), BF16),
                pltpu.VMEM((heads, width, 2 * HEAD_DIM), BF16),
                pltpu.VMEM((heads, length), jnp.int32),
                pltpu.VMEM((WINDOW + length, 2 * cols), BF16),
                pltpu.VMEM((groups, cols, width), BF16),
                pltpu.VMEM((groups, length, cols), BF16),
                pltpu.VMEM((length, width), BF16),
                pltpu.VMEM((length, width), BF16),
                pltpu.VMEM((heads, slots, length), BF16),
                pltpu.VMEM((heads, length, slots), BF16),
                pltpu.VMEM((heads, slots, 2 * HEAD_DIM), BF16),
                pltpu.VMEM((most, 2 * HEAD_DIM), BF16),
                pltpu.VMEM((HEAD_DIM, most), BF16),
                pltpu.VMEM((most, HEAD_DIM), BF16),
                pltpu.VMEM((heads, slots, HEAD_DIM), BF16),
                pltpu.VMEM((groups, length, cols), BF16),
                pltpu.VMEM((groups, cols, cols), BF16),
                dma((2, 2)), dma((2, 9)), dma((2, 4, 3)), dma((2, 3)),
                dma((wide_n,)), dma((wide_n,)), dma((wide_n,)), dma((wide_n,)),
                dma((2, 4, 3)), dma, dma((6 + 2 * heads,)),
            ],
            compiler_params=pltpu.CompilerParams(
                collective_id=0, has_side_effects=True, vmem_limit_bytes=56 * 1024 * 1024),
        )(tokens, w_qk1, w_value1, w_out1, w_qk2, w_value2, w_out2, cluster_ids)

    placed = (
        P("wide", None),
        P(None, "narrow"),
        P(None, "narrow"),
        P("narrow", None),
        P(None, "narrow"),
        P(None, "narrow"),
        P("narrow", None),
        P("narrow", "wide"),
    )
    return jax.shard_map(
        shards, mesh=mesh, in_specs=placed, out_specs=P("wide", "narrow"), check_vma=False
    )
```

```python
import functools
import math

import jax
import jax.numpy as jnp
from jax import lax
from jax.experimental import pallas as pl
from jax.experimental.pallas import tpu as pltpu
from jax.sharding import PartitionSpec as P

HEAD_DIM = 128
WINDOW = 256
EPS = 1e-06
BLOCK = 256
PIECE = 128
SCALE = math.log2(math.e) / math.sqrt(HEAD_DIM)
LOW = -1e30
MESH = pl.DeviceIdType.MESH
F32 = jnp.float32
BF16 = jnp.bfloat16


def flip(index, bit):
    return index + bit - 2 * bit * lax.rem(lax.div(index, bit), 2)


def rms_round(rows):
    values = rows.astype(F32)
    factor = lax.rsqrt(jnp.mean(values * values, axis=-1, keepdims=True) + EPS)
    return (values * factor).astype(BF16)


def dot(a, b):
    return jnp.dot(a, b, preferred_element_type=F32)


def dot_nt(a, b):
    return lax.dot_general(a, b, (((1,), (1,)), ((), ())), preferred_element_type=F32)


def dot_tn(a, b):
    return lax.dot_general(a, b, (((0,), (0,)), ((), ())), preferred_element_type=F32)


def send(src, dst, send_sem, recv_sem, **where):
    return pltpu.make_async_remote_copy(
        src_ref=src, dst_ref=dst, send_sem=send_sem, recv_sem=recv_sem,
        device_id=where, device_id_type=MESH)


def whole_kernel(wide_n, heads, clusters, sizes, pads, slots,
                 tokens_in, w_qk1, w_value1, w_out1, w_qk2, w_value2, w_out2, ids_in, out,
                 tokens, wkv1, wkv2, ids, kvx, w1, att1, hidden, normed2, to_slot, to_token, packed, arrived, value_t, answers, ret, before, w2,
                 halo_sem, w1_sems, att1_sems, w2_sems, go_s, go_r, back_s, back_r, att2_sems, local_sem, load_sems, ids_sems):
    me, n = lax.axis_index("wide"), lax.axis_index("narrow")
    near, far = flip(n, 1), flip(n, 2)
    cross = flip(near, 2)
    length = tokens_in.shape[0]
    cols = w_qk1.shape[1]
    counts = (clusters // 4, clusters // 2, clusters // 4)
    starts = (0, clusters // 4, 3 * clusters // 4)
    bases = (0, counts[0] * pads[0], counts[0] * pads[0] + counts[1] * pads[1])
    core = lax.rem(n, 2)

    def shuffle(place):
        low = flip(place, 2)
        high = flip(place, 1)
        return jnp.where(place < wide_n // 2, low, high)

    def flip_core(place):
        return jnp.where(core == 1, flip(place, 1), place)

    def device_of(owner):
        return flip_core(shuffle(owner))

    mine = shuffle(flip_core(me))
    my_head, my_rank = lax.div(mine, clusters), lax.rem(mine, clusters)

    barrier = pltpu.get_barrier_semaphore()

    @pl.loop(1, wide_n)
    def _(k):
        pl.semaphore_signal(barrier, inc=1, device_id={"wide": lax.rem(me + k, wide_n)}, device_id_type=MESH)

    for other in (near, far, cross):
        pl.semaphore_signal(barrier, inc=1, device_id={"narrow": other}, device_id_type=MESH)

    mine_cols = pl.ds(pl.multiple_of(n * cols, cols), cols)
    loads = [(tokens_in, tokens), (w_qk1, wkv1.at[:, pl.ds(0, cols)]), (w_value1, wkv1.at[:, pl.ds(cols, cols)]),
             (ids_in, ids.at[n]), (w_out1, w1.at[n]), (w_out2.at[:, mine_cols], w2.at[n])]
    for h in range(heads):
        part = pl.ds(h * HEAD_DIM, HEAD_DIM)
        loads.append((w_qk2.at[:, part], wkv2.at[h, :, pl.ds(0, HEAD_DIM)]))
        loads.append((w_value2.at[:, part], wkv2.at[h, :, pl.ds(HEAD_DIM, HEAD_DIM)]))
    loads = [pltpu.make_async_copy(src, dst, load_sems.at[index]) for index, (src, dst) in enumerate(loads)]
    for copy in loads:
        copy.start()

    def project1(start):
        rows = pl.ds(start, BLOCK)
        normed = rms_round(tokens[rows, :])
        there = pl.ds(WINDOW + start, BLOCK)
        kvx[there, :] = dot(normed, wkv1[...]).astype(BF16)

    tail = length - BLOCK
    quarter = cols // 4
    beside = flip(me, 2)
    parity = lax.rem(lax.div(me, 2), 2)
    early = [pl.ds(pl.multiple_of((2 * parity + c) * quarter, quarter), quarter) for c in range(2)]
    late = [pl.ds(pl.multiple_of((2 - 2 * parity + c) * quarter, quarter), quarter) for c in range(2)]
    w1_far = [send(w_out1.at[early[c]], w1.at[n, early[c]], w1_sems.at[0, c], w1_sems.at[1, c], narrow=far)
              for c in range(2)]
    w1_near = send(w_out1, w1.at[n], w1_sems.at[0, 2], w1_sems.at[1, 2], narrow=near)
    w1_swap = [send(w1.at[far, early[c]], w1.at[far, early[c]], w1_sems.at[0, 3 + c], w1_sems.at[1, 3 + c],
                    wide=beside) for c in range(2)]
    w1_fwd = [send(w1.at[far, rows], w1.at[far, rows], w1_sems.at[0, 5 + c], w1_sems.at[1, 5 + c], narrow=near)
              for c, rows in enumerate(early + late)]
    halo = [send(kvx.at[pl.ds(length + start, PIECE)], kvx.at[pl.ds(start, PIECE)], halo_sem.at[0, c],
                 halo_sem.at[1, c], wide=lax.rem(me + 1, wide_n)) for c, start in enumerate((PIECE, 0))]
    pl.semaphore_wait(barrier, wide_n - 1 + 3)
    for copy in w1_far:
        copy.start()
    ids_sends = [send(ids_in, ids.at[n], ids_sems.at[0, index], ids_sems.at[1, index], narrow=other)
                 for index, other in enumerate((near, far, cross))]
    for copy in ids_sends:
        copy.start()
    for copy in loads[:3]:
        copy.wait()
    project1(tail)

    @pl.when(me < wide_n - 1)
    def _():
        for copy in halo:
            copy.start()

    w1_near.start()

    @pl.when(me == 0)
    def _():
        kvx[pl.ds(0, WINDOW), :] = jnp.zeros((WINDOW, 2 * cols), BF16)

    project1(0)

    def window(start):
        key_at = lax.broadcasted_iota(jnp.int32, (WINDOW + PIECE, PIECE), 0) + (me * length + start - WINDOW)
        query_at = lax.broadcasted_iota(jnp.int32, (WINDOW + PIECE, PIECE), 1) + (me * length + start)
        gap = query_at - key_at
        keep = (gap > 0) & (gap < WINDOW) & (key_at >= 0) | (gap == 0) & (query_at == 0)
        for h in range(heads):
            q = kvx[pl.ds(start + WINDOW, PIECE), pl.ds(h * HEAD_DIM, HEAD_DIM)]
            k = kvx[pl.ds(start, WINDOW + PIECE), pl.ds(h * HEAD_DIM, HEAD_DIM)]
            v = kvx[pl.ds(start, WINDOW + PIECE), pl.ds(cols + h * HEAD_DIM, HEAD_DIM)]
            scores = jnp.where(keep, dot_nt(k, q) * SCALE, LOW)
            top = jnp.max(scores, axis=0, keepdims=True)
            weights = jnp.exp2(scores - top)
            total = jnp.sum(weights, axis=0, keepdims=True)
            mixed = dot_tn(v, weights.astype(BF16)) / total
            att1[n, pl.ds(start, PIECE), pl.ds(h * HEAD_DIM, HEAD_DIM)] = mixed.T.astype(BF16)

    def share(buffer, sems, half, size):
        rows = pl.ds(half * size, size)
        first = send(buffer.at[n, rows], buffer.at[n, rows], sems.at[0, half, 0], sems.at[1, half, 0], narrow=far)
        second = send(buffer.at[n, rows], buffer.at[n, rows], sems.at[0, half, 1], sems.at[1, half, 1], narrow=near)
        third = send(buffer.at[far, rows], buffer.at[far, rows], sems.at[0, half, 2], sems.at[1, half, 2],
                     narrow=near)
        return first, second, third

    att1_sends = [share(att1, att1_sems, part, PIECE) for part in range(4)]
    def attend_window(part):
        window(part * PIECE)
        att1_sends[part][0].start()
        att1_sends[part][1].start()

    attend_window(3)
    attend_window(2)
    most = 128
    before[...] = (lax.broadcasted_iota(jnp.int32, (length, length), 0)
              <= lax.broadcasted_iota(jnp.int32, (length, length), 1)).astype(F32).astype(BF16)

    def slot_of(g, h):
        match = (lax.broadcasted_iota(jnp.int32, (most, length), 0) == ids[g, pl.ds(h, 1), :]).astype(F32)
        match16 = match.astype(BF16)
        running = dot(match16, before[...])
        held = jnp.sum(match, axis=1, keepdims=True)
        held_row = dot_nt(jnp.ones((8, length), BF16), match16)[0:1, :]
        lower = (lax.broadcasted_iota(jnp.int32, (most, most), 1)
                 < lax.broadcasted_iota(jnp.int32, (most, most), 0))
        ahead = (held_row > held) | (held_row == held) & lower
        rank = jnp.sum(ahead.astype(F32), axis=1, keepdims=True)
        base = jnp.where(
            rank < starts[1], rank * pads[0],
            jnp.where(rank < starts[2], bases[1] + (rank - starts[1]) * pads[1],
                      bases[2] + (rank - starts[2]) * pads[2]))
        target = jnp.sum(match * (base + running - 1.0), axis=0, keepdims=True)
        target_col = jnp.broadcast_to(target, (8, length)).T[:, 0:1].astype(jnp.int32)
        target = target.astype(jnp.int32)
        to_token[g, h] = (lax.broadcasted_iota(jnp.int32, (length, slots), 1) == target_col).astype(F32).astype(BF16)
        return target

    def own_slots(h):
        target = slot_of(n, h)
        to_slot[h] = (lax.broadcasted_iota(jnp.int32, (slots, length), 0) == target).astype(F32).astype(BF16)

    loads[3].wait()
    for c in range(2):
        w1_far[c].wait_recv()
        w1_swap[c].start()
        w1_fwd[c].start()
        if c < heads:
            own_slots(c)
    for h in range(2, heads):
        own_slots(h)

    for part in (1, 0):
        @pl.when(me > 0)
        def _():
            halo[1 - part].wait_recv()

        attend_window(part)

    def forward(part):
        att1_sends[part][0].wait_recv()
        att1_sends[part][2].start()

    forward(3)
    forward(2)
    w1_swap[0].wait_recv()
    w1_fwd[2].start()
    forward(1)
    w1_swap[1].wait_recv()
    w1_fwd[3].start()
    for copy in loads[4:]:
        copy.wait()
    w1_near.wait_recv()
    for copy in w1_fwd:
        copy.wait_recv()

    def rest(parts):
        for part in parts:
            att1_sends[part][1].wait_recv()
            att1_sends[part][2].wait_recv()
        rows = pl.ds(parts[-1] * PIECE, len(parts) * PIECE)
        total = tokens[rows, :].astype(F32)
        for g in range(4):
            total = total + dot(att1[g, rows, :], w1[g])
        hidden16 = total.astype(BF16)
        hidden[rows, :] = hidden16
        normed2[rows, :] = rms_round(hidden16)

    rest((3, 2))
    forward(0)
    rest((1, 0))

    def place(level, head, step):
        rank = starts[level] + step
        owner = head * clusters + rank
        offset = pl.multiple_of(bases[level] + step * pads[level], 16)
        return owner, device_of(owner), offset

    def go(level, head, step):
        owner, there, offset = place(level, head, step)
        size = pads[level]
        return there, send(packed.at[head, pl.ds(offset, size)],
                           arrived.at[pl.ds(pl.multiple_of(me * size, 16), size)],
                           go_s.at[owner], go_r.at[me], wide=there), (head, offset, size)

    def each_owner(body):
        for level in range(3):
            @pl.loop(0, heads * counts[level])
            def _(item):
                body(level, lax.div(item, counts[level]), lax.rem(item, counts[level]))

    def start_go(level, head, step):
        there, copy, (_, offset, size) = go(level, head, step)

        @pl.when(there != me)
        def _():
            copy.start()

        @pl.when(there == me)
        def _():
            own = pltpu.make_async_copy(packed.at[head, pl.ds(offset, size)],
                                        arrived.at[pl.ds(pl.multiple_of(me * size, 16), size)], local_sem)
            own.start()
            own.wait()

    def leave(level, head):
        @pl.loop(0, counts[level])
        def _(step):
            start_go(level, head, step)

    order = [lax.rem(turn + jnp.where(me < wide_n // 2, 1, 0), heads) for turn in range(heads)]
    for h in order:
        packed[h] = dot(to_slot[h], dot(normed2[...], wkv2[h]).astype(BF16)).astype(BF16)
        leave(0, h)
    for level in (1, 2):
        for h in order:
            leave(level, h)

    w2_sends = []
    for index, other in enumerate((near, far, cross)):
        w2_sends.append(send(w_out2.at[:, pl.ds(pl.multiple_of(other * cols, cols), cols)], w2.at[n],
                             w2_sems.at[0, index], w2_sems.at[1, index], narrow=other))
        w2_sends[-1].start()

    for copy in ids_sends:
        copy.wait_recv()
    for g in (near, far, cross):
        for h in range(heads):
            slot_of(g, h)

    def for_level(body):
        for level in range(3):
            @pl.when((my_rank >= starts[level]) & (my_rank < starts[level] + counts[level]))
            def _():
                body(level)

    def from_source(level, source):
        size = pads[level]
        rows = pl.ds(pl.multiple_of(source * size, 16), size)
        return send(packed.at[0, pl.ds(0, size)], arrived.at[rows], go_s.at[0], go_r.at[source], wide=source)

    def back_copy(level, source):
        size = pads[level]
        rows = pl.ds(pl.multiple_of(source * size, 16), size)
        offset = pl.multiple_of(bases[level] + (my_rank - starts[level]) * size, 16)
        return rows, offset, send(answers.at[rows], ret.at[n, my_head, pl.ds(offset, size)],
                                  back_s.at[source], back_r.at[mine], wide=source)

    def receive(level, source):
        @pl.when(source != me)
        def _():
            from_source(level, source).wait_recv()

    def give_back(level, source):
        rows, offset, copy = back_copy(level, source)

        @pl.when(source != me)
        def _():
            copy.start()

        @pl.when(source == me)
        def _():
            own = pltpu.make_async_copy(answers.at[rows], ret.at[n, my_head, pl.ds(offset, pads[level])], local_sem)
            own.start()
            own.wait()

    def attend(level, block):
        size, real = pads[level], sizes[level]
        begin = block * BLOCK
        here = pl.ds(begin, BLOCK)
        q = arrived[here, pl.ds(0, HEAD_DIM)]
        value_t[:, here] = arrived[here, pl.ds(HEAD_DIM, HEAD_DIM)].T

        def score(first, rows, diagonal):
            scores = dot_nt(arrived[pl.ds(first, rows), pl.ds(0, HEAD_DIM)], q) * SCALE
            keep = None
            key_at = lax.broadcasted_iota(jnp.int32, (rows, BLOCK), 0)
            if diagonal:
                query_at = lax.broadcasted_iota(jnp.int32, (rows, BLOCK), 1)
                keep = key_at < query_at
                if block == 0:
                    keep = keep | (key_at + query_at == 0)
            if size != real:
                live = lax.rem(key_at + first, size) < real
                keep = live if keep is None else keep & live
            return scores if keep is None else jnp.where(keep, scores, LOW)

        parts = [(begin, score(begin, BLOCK, True))]
        if block > 0:
            parts.append((0, score(0, begin, False)))
        top = functools.reduce(jnp.maximum, [jnp.max(scores, axis=0, keepdims=True) for _, scores in parts])
        total, mixed = 0.0, 0.0
        for first, scores in parts:
            weights = jnp.exp2(scores - top)
            total = total + jnp.sum(weights, axis=0, keepdims=True)
            mixed = mixed + dot(value_t[:, pl.ds(first, scores.shape[0])], weights.astype(BF16))
        answers[here, :] = (mixed / total).T.astype(BF16)

    def own_clusters(level):
        size = pads[level]
        came, gone = 0, 0
        for block in range(wide_n * size // BLOCK):
            end = (block + 1) * BLOCK

            @pl.loop(came, -(-end // size))
            def _(source):
                receive(level, source)

            attend(level, block)

            @pl.loop(gone, end // size)
            def _(source):
                give_back(level, source)

            came, gone = -(-end // size), end // size

    for_level(own_clusters)

    def wait_back(level, head, step):
        owner, there, offset = place(level, head, step)
        size = pads[level]

        @pl.when(there != me)
        def _():
            send(answers.at[pl.ds(0, size)], ret.at[n, head, pl.ds(offset, size)],
                 back_s.at[0], back_r.at[owner], wide=there).wait_recv()

    spans = ((0, bases[1]), (bases[1], slots - bases[1]))
    att2_sends = []
    for start, size in spans:
        for h in range(heads):
            rows = pl.ds(start, size)
            index = len(att2_sends)
            own, other = ret.at[n, h, rows], ret.at[far, h, rows]
            att2_sends.append((
                send(own, own, att2_sems.at[0, index, 0], att2_sems.at[1, index, 0], narrow=far),
                send(own, own, att2_sems.at[0, index, 1], att2_sems.at[1, index, 1], narrow=near),
                send(other, other, att2_sems.at[0, index, 2], att2_sems.at[1, index, 2], narrow=near)))
    for span, levels in enumerate(((0,), (1, 2))):
        for h in range(heads):
            for level in levels:
                @pl.loop(0, counts[level])
                def _(step):
                    wait_back(level, h, step)
            att2_sends[span * heads + h][0].start()
            att2_sends[span * heads + h][1].start()

    def result(g):
        for half in range(length // BLOCK):
            rows = pl.ds(half * BLOCK, BLOCK)
            mixed = jnp.concatenate([dot(to_token[g, h, rows, :], ret[g, h]).astype(BF16) for h in range(heads)], axis=1)
            out[rows, :] += dot(mixed, w2[g])

    out[...] = hidden[:, mine_cols].astype(F32)
    for copy in w2_sends:
        copy.wait_recv()
    result(n)
    for first, second, third in att2_sends:
        first.wait_recv()
        third.start()
    for first, second, third in att2_sends:
        second.wait_recv()
    result(near)
    result(far)
    for first, second, third in att2_sends:
        third.wait_recv()
    result(cross)

    for copy in (*w1_far, w1_near, *w1_swap, *w1_fwd, *w2_sends, *ids_sends,
                 *(copy for copies in att1_sends + att2_sends for copy in copies)):
        copy.wait_send()

    @pl.when(me < wide_n - 1)
    def _():
        for copy in halo:
            copy.wait_send()

    def sent(level, head, step):
        there, copy, _ = go(level, head, step)

        @pl.when(there != me)
        def _():
            copy.wait_send()

    each_owner(sent)

    def sent_back(level):
        @pl.loop(0, wide_n)
        def _(source):
            @pl.when(source != me)
            def _():
                back_copy(level, source)[2].wait_send()

    for_level(sent_back)


def hand_on(answer, out):
    out[...] = answer[...]


def solution(mesh):
    wide_n = mesh.shape["wide"]

    def shards(tokens, w_qk1, w_value1, w_out1, w_qk2, w_value2, w_out2, cluster_ids):
        length, width = tokens.shape
        cols = w_qk1.shape[1]
        heads = cols // HEAD_DIM
        clusters = wide_n // heads
        cap = 2 * length * heads // wide_n
        sizes = (cap, 3 * cap // 8, cap // 4)
        pads = tuple(-(-size // 16) * 16 for size in sizes)
        slots = clusters // 4 * pads[0] + clusters // 2 * pads[1] + clusters // 4 * pads[2]
        most = wide_n * pads[0]
        groups = mesh.shape["narrow"]
        dma = pltpu.SemaphoreType.DMA
        vmem = pl.BlockSpec(memory_space=pltpu.VMEM)
        answer = pl.pallas_call(
            functools.partial(whole_kernel, wide_n, heads, clusters, sizes, pads, slots),
            out_shape=jax.ShapeDtypeStruct((length, cols), F32),
            in_specs=[pl.BlockSpec(memory_space=pl.ANY)] * 8,
            out_specs=vmem,
            scratch_shapes=[
                pltpu.VMEM((length, width), BF16),
                pltpu.VMEM((width, 2 * cols), BF16),
                pltpu.VMEM((heads, width, 2 * HEAD_DIM), BF16),
                pltpu.VMEM((groups, heads, length), jnp.int32),
                pltpu.VMEM((WINDOW + length, 2 * cols), BF16),
                pltpu.VMEM((groups, cols, width), BF16),
                pltpu.VMEM((groups, length, cols), BF16),
                pltpu.VMEM((length, width), BF16),
                pltpu.VMEM((length, width), BF16),
                pltpu.VMEM((heads, slots, length), BF16),
                pltpu.VMEM((groups, heads, length, slots), BF16),
                pltpu.VMEM((heads, slots, 2 * HEAD_DIM), BF16),
                pltpu.VMEM((most, 2 * HEAD_DIM), BF16),
                pltpu.VMEM((HEAD_DIM, most), BF16),
                pltpu.VMEM((most, HEAD_DIM), BF16),
                pltpu.VMEM((groups, heads, slots, HEAD_DIM), BF16),
                pltpu.VMEM((length, length), BF16),
                pltpu.VMEM((groups, cols, cols), BF16),
                dma((2, 2)), dma((2, 9)), dma((2, 4, 3)), dma((2, 3)),
                dma((wide_n,)), dma((wide_n,)), dma((wide_n,)), dma((wide_n,)),
                dma((2, 2 * heads, 3)), dma, dma((6 + 2 * heads,)), dma((2, 3)),
            ],
            compiler_params=pltpu.CompilerParams(
                collective_id=0, has_side_effects=True, vmem_limit_bytes=56 * 1024 * 1024),
        )(tokens, w_qk1, w_value1, w_out1, w_qk2, w_value2, w_out2, cluster_ids)
        return pl.pallas_call(
            hand_on,
            grid=(2,),
            out_shape=jax.ShapeDtypeStruct((length, cols), F32),
            in_specs=[pl.BlockSpec((length // 2, cols), lambda i: (i, 0))],
            out_specs=pl.BlockSpec((length // 2, cols), lambda i: (i, 0)),
        )(answer)

    placed = (
        P("wide", None),
        P(None, "narrow"),
        P(None, "narrow"),
        P("narrow", None),
        P(None, "narrow"),
        P(None, "narrow"),
        P("narrow", None),
        P("narrow", "wide"),
    )
    return jax.shard_map(
        shards, mesh=mesh, in_specs=placed, out_specs=P("wide", "narrow"), check_vma=False
    )
```

```python
import functools
import math

import jax
import jax.numpy as jnp
from jax import lax
from jax.experimental import pallas as pl
from jax.experimental.pallas import tpu as pltpu
from jax.sharding import PartitionSpec as P

HEAD_DIM = 128
WINDOW = 256
EPS = 1e-06
BLOCK = 256
PIECE = 128
SCALE = math.log2(math.e) / math.sqrt(HEAD_DIM)
LOW = -1e30
MESH = pl.DeviceIdType.MESH
F32 = jnp.float32
BF16 = jnp.bfloat16


def flip(index, bit):
    return index + bit - 2 * bit * lax.rem(lax.div(index, bit), 2)


def rms_round(rows):
    values = rows.astype(F32)
    factor = lax.rsqrt(jnp.mean(values * values, axis=-1, keepdims=True) + EPS)
    return (values * factor).astype(BF16)


def dot(a, b):
    return jnp.dot(a, b, preferred_element_type=F32)


def dot_nt(a, b):
    return lax.dot_general(a, b, (((1,), (1,)), ((), ())), preferred_element_type=F32)


def dot_tn(a, b):
    return lax.dot_general(a, b, (((0,), (0,)), ((), ())), preferred_element_type=F32)


def scaled(q):
    return (q.astype(F32) * SCALE).astype(BF16)


def send(src, dst, send_sem, recv_sem, **where):
    return pltpu.make_async_remote_copy(
        src_ref=src, dst_ref=dst, send_sem=send_sem, recv_sem=recv_sem,
        device_id=where, device_id_type=MESH)


def whole_kernel(wide_n, heads, clusters, sizes, pads, slots,
                 tokens_in, w_qk1, w_value1, w_out1, w_qk2, w_value2, w_out2, ids_in, out,
                 tokens, wkv1, wkv2, ids, places, kvx, w1, att1, hidden, normed2, to_slot, to_token, packed, arrived, value_t, answers, ret, before, w2,
                 halo_sem, w1_sems, att1_sems, w2_sems, go_s, go_r, back_s, back_r, att2_sems, local_sem, load_sems, ids_sems):
    me, n = lax.axis_index("wide"), lax.axis_index("narrow")
    near, far = flip(n, 1), flip(n, 2)
    cross = flip(near, 2)
    length = tokens_in.shape[0]
    cols = w_qk1.shape[1]
    counts = (clusters // 4, clusters // 2, clusters // 4)
    starts = (0, clusters // 4, 3 * clusters // 4)
    bases = (0, counts[0] * pads[0], counts[0] * pads[0] + counts[1] * pads[1])
    core = lax.rem(n, 2)

    def shuffle(place):
        low = flip(place, 2)
        high = flip(place, 1)
        return jnp.where(place < wide_n // 2, low, high)

    def flip_core(place):
        return jnp.where(core == 1, flip(place, 1), place)

    def device_of(owner):
        return flip_core(shuffle(owner))

    mine = shuffle(flip_core(me))
    my_head, my_rank = lax.div(mine, clusters), lax.rem(mine, clusters)

    barrier = pltpu.get_barrier_semaphore()

    @pl.loop(1, wide_n)
    def _(k):
        pl.semaphore_signal(barrier, inc=1, device_id={"wide": lax.rem(me + k, wide_n)}, device_id_type=MESH)

    for other in (near, far, cross):
        pl.semaphore_signal(barrier, inc=1, device_id={"narrow": other}, device_id_type=MESH)

    mine_cols = pl.ds(pl.multiple_of(n * cols, cols), cols)
    loads = [(tokens_in, tokens), (w_qk1, wkv1.at[:, pl.ds(0, cols)]), (w_value1, wkv1.at[:, pl.ds(cols, cols)]),
             (ids_in, ids), (w_out1, w1.at[n]), (w_out2.at[:, mine_cols], w2.at[n])]
    for h in range(heads):
        part = pl.ds(h * HEAD_DIM, HEAD_DIM)
        loads.append((w_qk2.at[:, part], wkv2.at[h, :, pl.ds(0, HEAD_DIM)]))
        loads.append((w_value2.at[:, part], wkv2.at[h, :, pl.ds(HEAD_DIM, HEAD_DIM)]))
    loads = [pltpu.make_async_copy(src, dst, load_sems.at[index]) for index, (src, dst) in enumerate(loads)]
    for copy in loads:
        copy.start()

    def project1(start):
        rows = pl.ds(start, BLOCK)
        normed = rms_round(tokens[rows, :])
        there = pl.ds(WINDOW + start, BLOCK)
        kvx[there, :] = dot(normed, wkv1[...]).astype(BF16)

    tail = length - BLOCK
    quarter = cols // 4
    beside = flip(me, 2)
    parity = lax.rem(lax.div(me, 2), 2)
    early = [pl.ds(pl.multiple_of((2 * parity + c) * quarter, quarter), quarter) for c in range(2)]
    late = [pl.ds(pl.multiple_of((2 - 2 * parity + c) * quarter, quarter), quarter) for c in range(2)]
    w1_far = [send(w_out1.at[early[c]], w1.at[n, early[c]], w1_sems.at[0, c], w1_sems.at[1, c], narrow=far)
              for c in range(2)]
    w1_near = send(w_out1, w1.at[n], w1_sems.at[0, 2], w1_sems.at[1, 2], narrow=near)
    w1_swap = [send(w1.at[far, early[c]], w1.at[far, early[c]], w1_sems.at[0, 3 + c], w1_sems.at[1, 3 + c],
                    wide=beside) for c in range(2)]
    w1_fwd = [send(w1.at[far, rows], w1.at[far, rows], w1_sems.at[0, 5 + c], w1_sems.at[1, 5 + c], narrow=near)
              for c, rows in enumerate(early + late)]
    halo = [send(kvx.at[pl.ds(length + start, PIECE)], kvx.at[pl.ds(start, PIECE)], halo_sem.at[0, c],
                 halo_sem.at[1, c], wide=lax.rem(me + 1, wide_n)) for c, start in enumerate((PIECE, 0))]
    pl.semaphore_wait(barrier, wide_n - 1 + 3)
    for copy in w1_far:
        copy.start()
    for copy in loads[:3]:
        copy.wait()
    project1(tail)

    @pl.when(me < wide_n - 1)
    def _():
        for copy in halo:
            copy.start()

    w1_near.start()

    @pl.when(me == 0)
    def _():
        kvx[pl.ds(0, WINDOW), :] = jnp.zeros((WINDOW, 2 * cols), BF16)

    project1(0)

    def window(start):
        key_at = lax.broadcasted_iota(jnp.int32, (WINDOW + PIECE, PIECE), 0) + (me * length + start - WINDOW)
        query_at = lax.broadcasted_iota(jnp.int32, (WINDOW + PIECE, PIECE), 1) + (me * length + start)
        gap = query_at - key_at
        keep = (gap > 0) & (gap < WINDOW) & (key_at >= 0) | (gap == 0) & (query_at == 0)
        for h in range(heads):
            q = kvx[pl.ds(start + WINDOW, PIECE), pl.ds(h * HEAD_DIM, HEAD_DIM)]
            k = kvx[pl.ds(start, WINDOW + PIECE), pl.ds(h * HEAD_DIM, HEAD_DIM)]
            v = kvx[pl.ds(start, WINDOW + PIECE), pl.ds(cols + h * HEAD_DIM, HEAD_DIM)]
            scores = jnp.where(keep, dot_nt(k, scaled(q)), LOW)
            top = jnp.max(scores, axis=0, keepdims=True)
            weights = jnp.exp2(scores - top)
            total = jnp.sum(weights, axis=0, keepdims=True)
            mixed = dot_tn(v, weights.astype(BF16)) / total
            att1[n, pl.ds(start, PIECE), pl.ds(h * HEAD_DIM, HEAD_DIM)] = mixed.T.astype(BF16)

    def share(buffer, sems, half, size):
        rows = pl.ds(half * size, size)
        first = send(buffer.at[n, rows], buffer.at[n, rows], sems.at[0, half, 0], sems.at[1, half, 0], narrow=far)
        second = send(buffer.at[n, rows], buffer.at[n, rows], sems.at[0, half, 1], sems.at[1, half, 1], narrow=near)
        third = send(buffer.at[far, rows], buffer.at[far, rows], sems.at[0, half, 2], sems.at[1, half, 2],
                     narrow=near)
        return first, second, third

    att1_sends = [share(att1, att1_sems, part, PIECE) for part in range(4)]
    def attend_window(part):
        window(part * PIECE)
        att1_sends[part][0].start()
        att1_sends[part][1].start()

    attend_window(3)
    attend_window(2)
    most = 128
    before[...] = (lax.broadcasted_iota(jnp.int32, (length, length), 0)
              <= lax.broadcasted_iota(jnp.int32, (length, length), 1)).astype(F32).astype(BF16)

    def slot_of(h):
        match = (lax.broadcasted_iota(jnp.int32, (most, length), 0) == ids[pl.ds(h, 1), :]).astype(F32)
        match16 = match.astype(BF16)
        running = dot(match16, before[...])
        held = jnp.sum(match, axis=1, keepdims=True)
        held_row = dot_nt(jnp.ones((8, length), BF16), match16)[0:1, :]
        lower = (lax.broadcasted_iota(jnp.int32, (most, most), 1)
                 < lax.broadcasted_iota(jnp.int32, (most, most), 0))
        ahead = (held_row > held) | (held_row == held) & lower
        rank = jnp.sum(ahead.astype(F32), axis=1, keepdims=True)
        base = jnp.where(
            rank < starts[1], rank * pads[0],
            jnp.where(rank < starts[2], bases[1] + (rank - starts[1]) * pads[1],
                      bases[2] + (rank - starts[2]) * pads[2]))
        target = jnp.sum(match * (base + running - 1.0), axis=0, keepdims=True)
        return target

    def token_matrix(g, h, target):
        target_col = jnp.broadcast_to(target, (8, length)).T[:, 0:1].astype(jnp.int32)
        to_token[g, h] = (lax.broadcasted_iota(jnp.int32, (length, slots), 1) == target_col).astype(F32).astype(BF16)

    def own_slots(h):
        target = slot_of(h)
        token_matrix(n, h, target)
        target = target.astype(jnp.int32)
        places[n, pl.ds(h, 1), :] = target
        to_slot[h] = (lax.broadcasted_iota(jnp.int32, (slots, length), 0) == target).astype(F32).astype(BF16)

    loads[3].wait()
    for c in range(2):
        w1_far[c].wait_recv()
        w1_swap[c].start()
        w1_fwd[c].start()
        if c < heads:
            own_slots(c)
    for h in range(2, heads):
        own_slots(h)
    ids_sends = [send(places.at[n], places.at[n], ids_sems.at[0, index], ids_sems.at[1, index], narrow=other)
                 for index, other in enumerate((near, far, cross))]
    for copy in ids_sends:
        copy.start()

    for part in (1, 0):
        @pl.when(me > 0)
        def _():
            halo[1 - part].wait_recv()

        attend_window(part)

    def forward(part):
        att1_sends[part][0].wait_recv()
        att1_sends[part][2].start()

    forward(3)
    forward(2)
    w1_swap[0].wait_recv()
    w1_fwd[2].start()
    forward(1)
    w1_swap[1].wait_recv()
    w1_fwd[3].start()
    for copy in loads[4:]:
        copy.wait()
    w1_near.wait_recv()
    for copy in w1_fwd:
        copy.wait_recv()

    def rest(parts):
        for part in parts:
            att1_sends[part][1].wait_recv()
            att1_sends[part][2].wait_recv()
        rows = pl.ds(parts[-1] * PIECE, len(parts) * PIECE)
        total = tokens[rows, :].astype(F32)
        for g in range(4):
            total = total + dot(att1[g, rows, :], w1[g])
        hidden16 = total.astype(BF16)
        hidden[rows, :] = hidden16
        normed2[rows, :] = rms_round(hidden16)

    rest((3, 2))
    forward(0)
    rest((1, 0))

    def place(level, head, step):
        rank = starts[level] + step
        owner = head * clusters + rank
        offset = pl.multiple_of(bases[level] + step * pads[level], 16)
        return owner, device_of(owner), offset

    def go(level, head, step):
        owner, there, offset = place(level, head, step)
        size = pads[level]
        return there, send(packed.at[head, pl.ds(offset, size)],
                           arrived.at[pl.ds(pl.multiple_of(me * size, 16), size)],
                           go_s.at[owner], go_r.at[me], wide=there), (head, offset, size)

    def each_owner(body):
        for level in range(3):
            @pl.loop(0, heads * counts[level])
            def _(item):
                body(level, lax.div(item, counts[level]), lax.rem(item, counts[level]))

    def start_go(level, head, step):
        there, copy, (_, offset, size) = go(level, head, step)

        @pl.when(there != me)
        def _():
            copy.start()

        @pl.when(there == me)
        def _():
            own = pltpu.make_async_copy(packed.at[head, pl.ds(offset, size)],
                                        arrived.at[pl.ds(pl.multiple_of(me * size, 16), size)], local_sem)
            own.start()
            own.wait()

    def leave(level, head):
        @pl.loop(0, counts[level])
        def _(step):
            start_go(level, head, step)

    order = [lax.rem(turn + jnp.where(me < wide_n // 2, 1, 0), heads) for turn in range(heads)]
    for h in order:
        packed[h] = dot(to_slot[h], dot(normed2[...], wkv2[h]).astype(BF16)).astype(BF16)
        leave(0, h)
    for level in (1, 2):
        for h in order:
            leave(level, h)

    w2_sends = []
    for index, other in enumerate((near, far, cross)):
        w2_sends.append(send(w_out2.at[:, pl.ds(pl.multiple_of(other * cols, cols), cols)], w2.at[n],
                             w2_sems.at[0, index], w2_sems.at[1, index], narrow=other))
        w2_sends[-1].start()

    for copy in ids_sends:
        copy.wait_recv()
    for g in (near, far, cross):
        for h in range(heads):
            token_matrix(g, h, places[g, pl.ds(h, 1), :].astype(F32))

    def for_level(body):
        for level in range(3):
            @pl.when((my_rank >= starts[level]) & (my_rank < starts[level] + counts[level]))
            def _():
                body(level)

    def from_source(level, source):
        size = pads[level]
        rows = pl.ds(pl.multiple_of(source * size, 16), size)
        return send(packed.at[0, pl.ds(0, size)], arrived.at[rows], go_s.at[0], go_r.at[source], wide=source)

    def back_copy(level, source):
        size = pads[level]
        rows = pl.ds(pl.multiple_of(source * size, 16), size)
        offset = pl.multiple_of(bases[level] + (my_rank - starts[level]) * size, 16)
        return rows, offset, send(answers.at[rows], ret.at[n, my_head, pl.ds(offset, size)],
                                  back_s.at[source], back_r.at[mine], wide=source)

    def receive(level, source):
        @pl.when(source != me)
        def _():
            from_source(level, source).wait_recv()

    def give_back(level, source):
        rows, offset, copy = back_copy(level, source)

        @pl.when(source != me)
        def _():
            copy.start()

        @pl.when(source == me)
        def _():
            own = pltpu.make_async_copy(answers.at[rows], ret.at[n, my_head, pl.ds(offset, pads[level])], local_sem)
            own.start()
            own.wait()

    def attend(level, block):
        size, real = pads[level], sizes[level]
        begin = block * BLOCK
        here = pl.ds(begin, BLOCK)
        q = scaled(arrived[here, pl.ds(0, HEAD_DIM)])
        value_t[:, here] = arrived[here, pl.ds(HEAD_DIM, HEAD_DIM)].T

        def score(first, rows, diagonal):
            scores = dot_nt(arrived[pl.ds(first, rows), pl.ds(0, HEAD_DIM)], q)
            keep = None
            key_at = lax.broadcasted_iota(jnp.int32, (rows, BLOCK), 0)
            if diagonal:
                query_at = lax.broadcasted_iota(jnp.int32, (rows, BLOCK), 1)
                keep = key_at < query_at
                if block == 0:
                    keep = keep | (key_at + query_at == 0)
            if size != real:
                live = lax.rem(key_at + first, size) < real
                keep = live if keep is None else keep & live
            return scores if keep is None else jnp.where(keep, scores, LOW)

        parts = [(begin, score(begin, BLOCK, True))]
        if block > 0:
            parts.append((0, score(0, begin, False)))
        top = functools.reduce(jnp.maximum, [jnp.max(scores, axis=0, keepdims=True) for _, scores in parts])
        total, mixed = 0.0, 0.0
        for first, scores in parts:
            weights = jnp.exp2(scores - top)
            total = total + jnp.sum(weights, axis=0, keepdims=True)
            mixed = mixed + dot(value_t[:, pl.ds(first, scores.shape[0])], weights.astype(BF16))
        answers[here, :] = (mixed / total).T.astype(BF16)

    def own_clusters(level):
        size = pads[level]
        came, gone = 0, 0
        for block in range(wide_n * size // BLOCK):
            end = (block + 1) * BLOCK

            @pl.loop(came, -(-end // size))
            def _(source):
                receive(level, source)

            attend(level, block)

            @pl.loop(gone, end // size)
            def _(source):
                give_back(level, source)

            came, gone = -(-end // size), end // size

    for_level(own_clusters)

    def wait_back(level, head, step):
        owner, there, offset = place(level, head, step)
        size = pads[level]

        @pl.when(there != me)
        def _():
            send(answers.at[pl.ds(0, size)], ret.at[n, head, pl.ds(offset, size)],
                 back_s.at[0], back_r.at[owner], wide=there).wait_recv()

    spans = ((0, bases[1]), (bases[1], slots - bases[1]))
    att2_sends = []
    for start, size in spans:
        for h in range(heads):
            rows = pl.ds(start, size)
            index = len(att2_sends)
            own, other = ret.at[n, h, rows], ret.at[far, h, rows]
            att2_sends.append((
                send(own, own, att2_sems.at[0, index, 0], att2_sems.at[1, index, 0], narrow=far),
                send(own, own, att2_sems.at[0, index, 1], att2_sems.at[1, index, 1], narrow=near),
                send(other, other, att2_sems.at[0, index, 2], att2_sems.at[1, index, 2], narrow=near)))
    for span, levels in enumerate(((0,), (1, 2))):
        for h in range(heads):
            for level in levels:
                @pl.loop(0, counts[level])
                def _(step):
                    wait_back(level, h, step)
            att2_sends[span * heads + h][0].start()
            att2_sends[span * heads + h][1].start()

    def result(g):
        for half in range(length // BLOCK):
            rows = pl.ds(half * BLOCK, BLOCK)
            mixed = jnp.concatenate([dot(to_token[g, h, rows, :], ret[g, h]).astype(BF16) for h in range(heads)], axis=1)
            out[rows, :] += dot(mixed, w2[g])

    out[...] = hidden[:, mine_cols].astype(F32)
    for copy in w2_sends:
        copy.wait_recv()
    result(n)
    for first, second, third in att2_sends:
        first.wait_recv()
        third.start()
    for first, second, third in att2_sends:
        second.wait_recv()
    result(near)
    result(far)
    for first, second, third in att2_sends:
        third.wait_recv()
    result(cross)

    for copy in (*w1_far, w1_near, *w1_swap, *w1_fwd, *w2_sends, *ids_sends,
                 *(copy for copies in att1_sends + att2_sends for copy in copies)):
        copy.wait_send()

    @pl.when(me < wide_n - 1)
    def _():
        for copy in halo:
            copy.wait_send()

    def sent(level, head, step):
        there, copy, _ = go(level, head, step)

        @pl.when(there != me)
        def _():
            copy.wait_send()

    each_owner(sent)

    def sent_back(level):
        @pl.loop(0, wide_n)
        def _(source):
            @pl.when(source != me)
            def _():
                back_copy(level, source)[2].wait_send()

    for_level(sent_back)


def hand_on(answer, out, sems):
    size = answer.shape[0] // 8
    copies = [pltpu.make_async_copy(answer.at[pl.ds(part * size, size)], out.at[pl.ds(part * size, size)], sems.at[part])
              for part in range(8)]
    for copy in copies:
        copy.start()
    for copy in copies:
        copy.wait()


def solution(mesh):
    wide_n = mesh.shape["wide"]

    def shards(tokens, w_qk1, w_value1, w_out1, w_qk2, w_value2, w_out2, cluster_ids):
        length, width = tokens.shape
        cols = w_qk1.shape[1]
        heads = cols // HEAD_DIM
        clusters = wide_n // heads
        cap = 2 * length * heads // wide_n
        sizes = (cap, 3 * cap // 8, cap // 4)
        pads = tuple(-(-size // 16) * 16 for size in sizes)
        slots = clusters // 4 * pads[0] + clusters // 2 * pads[1] + clusters // 4 * pads[2]
        most = wide_n * pads[0]
        groups = mesh.shape["narrow"]
        dma = pltpu.SemaphoreType.DMA
        vmem = pl.BlockSpec(memory_space=pltpu.VMEM)
        answer = pl.pallas_call(
            functools.partial(whole_kernel, wide_n, heads, clusters, sizes, pads, slots),
            out_shape=jax.ShapeDtypeStruct((length, cols), F32),
            in_specs=[pl.BlockSpec(memory_space=pl.ANY)] * 8,
            out_specs=vmem,
            scratch_shapes=[
                pltpu.VMEM((length, width), BF16),
                pltpu.VMEM((width, 2 * cols), BF16),
                pltpu.VMEM((heads, width, 2 * HEAD_DIM), BF16),
                pltpu.VMEM((heads, length), jnp.int32),
                pltpu.VMEM((groups, heads, length), jnp.int32),
                pltpu.VMEM((WINDOW + length, 2 * cols), BF16),
                pltpu.VMEM((groups, cols, width), BF16),
                pltpu.VMEM((groups, length, cols), BF16),
                pltpu.VMEM((length, width), BF16),
                pltpu.VMEM((length, width), BF16),
                pltpu.VMEM((heads, slots, length), BF16),
                pltpu.VMEM((groups, heads, length, slots), BF16),
                pltpu.VMEM((heads, slots, 2 * HEAD_DIM), BF16),
                pltpu.VMEM((most, 2 * HEAD_DIM), BF16),
                pltpu.VMEM((HEAD_DIM, most), BF16),
                pltpu.VMEM((most, HEAD_DIM), BF16),
                pltpu.VMEM((groups, heads, slots, HEAD_DIM), BF16),
                pltpu.VMEM((length, length), BF16),
                pltpu.VMEM((groups, cols, cols), BF16),
                dma((2, 2)), dma((2, 9)), dma((2, 4, 3)), dma((2, 3)),
                dma((wide_n,)), dma((wide_n,)), dma((wide_n,)), dma((wide_n,)),
                dma((2, 2 * heads, 3)), dma, dma((6 + 2 * heads,)), dma((2, 3)),
            ],
            compiler_params=pltpu.CompilerParams(
                collective_id=0, has_side_effects=True, vmem_limit_bytes=56 * 1024 * 1024),
        )(tokens, w_qk1, w_value1, w_out1, w_qk2, w_value2, w_out2, cluster_ids)
        return pl.pallas_call(
            hand_on,
            out_shape=jax.ShapeDtypeStruct((length, cols), F32),
            in_specs=[pl.BlockSpec(memory_space=pl.ANY)],
            out_specs=pl.BlockSpec(memory_space=pl.ANY),
            scratch_shapes=[dma((8,))],
        )(answer)

    placed = (
        P("wide", None),
        P(None, "narrow"),
        P(None, "narrow"),
        P("narrow", None),
        P(None, "narrow"),
        P(None, "narrow"),
        P("narrow", None),
        P("narrow", "wide"),
    )
    return jax.shard_map(
        shards, mesh=mesh, in_specs=placed, out_specs=P("wide", "narrow"), check_vma=False
    )
```

```python
import functools
import math

import jax
import jax.numpy as jnp
from jax import lax
from jax.experimental import pallas as pl
from jax.experimental.pallas import tpu as pltpu
from jax.sharding import PartitionSpec as P

HEAD_DIM = 128
WINDOW = 256
EPS = 1e-06
BLOCK = 256
PIECE = 128
SCALE = math.log2(math.e) / math.sqrt(HEAD_DIM)
LOW = -1e30
MESH = pl.DeviceIdType.MESH
F32 = jnp.float32
BF16 = jnp.bfloat16


def flip(index, bit):
    return index + bit - 2 * bit * lax.rem(lax.div(index, bit), 2)


def rms_round(rows):
    values = rows.astype(F32)
    factor = lax.rsqrt(jnp.mean(values * values, axis=-1, keepdims=True) + EPS)
    return (values * factor).astype(BF16)


def dot(a, b):
    return jnp.dot(a, b, preferred_element_type=F32)


def dot_nt(a, b):
    return lax.dot_general(a, b, (((1,), (1,)), ((), ())), preferred_element_type=F32)


def dot_tn(a, b):
    return lax.dot_general(a, b, (((0,), (0,)), ((), ())), preferred_element_type=F32)


def scaled(q):
    return (q.astype(F32) * SCALE).astype(BF16)


def send(src, dst, send_sem, recv_sem, **where):
    return pltpu.make_async_remote_copy(
        src_ref=src, dst_ref=dst, send_sem=send_sem, recv_sem=recv_sem,
        device_id=where, device_id_type=MESH)


def whole_kernel(wide_n, heads, clusters, sizes, pads, slots,
                 tokens_in, w_qk1, w_value1, w_out1, w_qk2, w_value2, w_out2, ids_in, out,
                 tokens, wkv1, wkv2, ids, places, kvx, w1, att1, hidden, normed2, to_slot, to_token, packed, arrived, value_t, answers, ret, before, w2,
                 halo_sem, w1_sems, att1_sems, w2_sems, go_s, go_r, back_s, back_r, att2_sems, local_sem, load_sems, ids_sems):
    me, n = lax.axis_index("wide"), lax.axis_index("narrow")
    near, far = flip(n, 1), flip(n, 2)
    cross = flip(near, 2)
    length = tokens_in.shape[0]
    cols = w_qk1.shape[1]
    counts = (clusters // 4, clusters // 2, clusters // 4)
    starts = (0, clusters // 4, 3 * clusters // 4)
    bases = (0, counts[0] * pads[0], counts[0] * pads[0] + counts[1] * pads[1])
    core = lax.rem(n, 2)

    def shuffle(place):
        low = flip(place, 2)
        high = flip(place, 1)
        return jnp.where(place < wide_n // 2, low, high)

    def flip_core(place):
        return jnp.where(core == 1, flip(place, 1), place)

    def device_of(owner):
        return flip_core(shuffle(owner))

    mine = shuffle(flip_core(me))
    my_head, my_rank = lax.div(mine, clusters), lax.rem(mine, clusters)

    barrier = pltpu.get_barrier_semaphore()

    @pl.loop(1, wide_n)
    def _(k):
        pl.semaphore_signal(barrier, inc=1, device_id={"wide": lax.rem(me + k, wide_n)}, device_id_type=MESH)

    for other in (near, far, cross):
        pl.semaphore_signal(barrier, inc=1, device_id={"narrow": other}, device_id_type=MESH)

    mine_cols = pl.ds(pl.multiple_of(n * cols, cols), cols)
    loads = [(tokens_in, tokens), (w_qk1, wkv1.at[:, pl.ds(0, cols)]), (w_value1, wkv1.at[:, pl.ds(cols, cols)]),
             (ids_in, ids), (w_out1, w1.at[n]), (w_out2.at[:, mine_cols], w2.at[n])]
    for h in range(heads):
        part = pl.ds(h * HEAD_DIM, HEAD_DIM)
        loads.append((w_qk2.at[:, part], wkv2.at[h, :, pl.ds(0, HEAD_DIM)]))
        loads.append((w_value2.at[:, part], wkv2.at[h, :, pl.ds(HEAD_DIM, HEAD_DIM)]))
    loads = [pltpu.make_async_copy(src, dst, load_sems.at[index]) for index, (src, dst) in enumerate(loads)]
    for copy in loads:
        copy.start()

    def project1(start):
        rows = pl.ds(start, BLOCK)
        normed = rms_round(tokens[rows, :])
        there = pl.ds(WINDOW + start, BLOCK)
        kvx[there, :] = dot(normed, wkv1[...]).astype(BF16)

    tail = length - BLOCK
    quarter = cols // 4
    beside = flip(me, 2)
    parity = lax.rem(lax.div(me, 2), 2)
    early = [pl.ds(pl.multiple_of((2 * parity + c) * quarter, quarter), quarter) for c in range(2)]
    late = [pl.ds(pl.multiple_of((2 - 2 * parity + c) * quarter, quarter), quarter) for c in range(2)]
    w1_far = [send(w_out1.at[early[c]], w1.at[n, early[c]], w1_sems.at[0, c], w1_sems.at[1, c], narrow=far)
              for c in range(2)]
    w1_near = send(w_out1, w1.at[n], w1_sems.at[0, 2], w1_sems.at[1, 2], narrow=near)
    w1_swap = [send(w1.at[far, early[c]], w1.at[far, early[c]], w1_sems.at[0, 3 + c], w1_sems.at[1, 3 + c],
                    wide=beside) for c in range(2)]
    w1_fwd = [send(w1.at[far, rows], w1.at[far, rows], w1_sems.at[0, 5 + c], w1_sems.at[1, 5 + c], narrow=near)
              for c, rows in enumerate(early + late)]
    halo = [send(kvx.at[pl.ds(length + start, PIECE)], kvx.at[pl.ds(start, PIECE)], halo_sem.at[0, c],
                 halo_sem.at[1, c], wide=lax.rem(me + 1, wide_n)) for c, start in enumerate((PIECE, 0))]
    pl.semaphore_wait(barrier, wide_n - 1 + 3)
    for copy in w1_far:
        copy.start()
    for copy in loads[:3]:
        copy.wait()
    project1(tail)

    @pl.when(me < wide_n - 1)
    def _():
        for copy in halo:
            copy.start()

    w1_near.start()

    @pl.when(me == 0)
    def _():
        kvx[pl.ds(0, WINDOW), :] = jnp.zeros((WINDOW, 2 * cols), BF16)

    project1(0)

    def window(start):
        key_at = lax.broadcasted_iota(jnp.int32, (WINDOW + PIECE, PIECE), 0) + (me * length + start - WINDOW)
        query_at = lax.broadcasted_iota(jnp.int32, (WINDOW + PIECE, PIECE), 1) + (me * length + start)
        gap = query_at - key_at
        keep = (gap > 0) & (gap < WINDOW) & (key_at >= 0) | (gap == 0) & (query_at == 0)
        for h in range(heads):
            q = kvx[pl.ds(start + WINDOW, PIECE), pl.ds(h * HEAD_DIM, HEAD_DIM)]
            k = kvx[pl.ds(start, WINDOW + PIECE), pl.ds(h * HEAD_DIM, HEAD_DIM)]
            v = kvx[pl.ds(start, WINDOW + PIECE), pl.ds(cols + h * HEAD_DIM, HEAD_DIM)]
            scores = jnp.where(keep, dot_nt(k, scaled(q)), LOW)
            top = jnp.max(scores, axis=0, keepdims=True)
            weights = jnp.exp2(scores - top)
            total = jnp.sum(weights, axis=0, keepdims=True)
            mixed = dot_tn(v, weights.astype(BF16)) / total
            att1[n, pl.ds(start, PIECE), pl.ds(h * HEAD_DIM, HEAD_DIM)] = mixed.T.astype(BF16)

    def share(buffer, sems, half, size):
        rows = pl.ds(half * size, size)
        first = send(buffer.at[n, rows], buffer.at[n, rows], sems.at[0, half, 0], sems.at[1, half, 0], narrow=far)
        second = send(buffer.at[n, rows], buffer.at[n, rows], sems.at[0, half, 1], sems.at[1, half, 1], narrow=near)
        third = send(buffer.at[far, rows], buffer.at[far, rows], sems.at[0, half, 2], sems.at[1, half, 2],
                     narrow=near)
        return first, second, third

    att1_sends = [share(att1, att1_sems, part, PIECE) for part in range(4)]
    def attend_window(part):
        window(part * PIECE)
        att1_sends[part][0].start()
        att1_sends[part][1].start()

    attend_window(3)
    attend_window(2)
    most = 128
    before[...] = (lax.broadcasted_iota(jnp.int32, (length, length), 0)
              <= lax.broadcasted_iota(jnp.int32, (length, length), 1)).astype(F32).astype(BF16)

    def slot_of(h):
        match = (lax.broadcasted_iota(jnp.int32, (most, length), 0) == ids[pl.ds(h, 1), :]).astype(F32)
        match16 = match.astype(BF16)
        running = dot(match16, before[...])
        held = jnp.sum(match, axis=1, keepdims=True)
        held_row = dot_nt(jnp.ones((8, length), BF16), match16)[0:1, :]
        lower = (lax.broadcasted_iota(jnp.int32, (most, most), 1)
                 < lax.broadcasted_iota(jnp.int32, (most, most), 0))
        ahead = (held_row > held) | (held_row == held) & lower
        rank = jnp.sum(ahead.astype(F32), axis=1, keepdims=True)
        base = jnp.where(
            rank < starts[1], rank * pads[0],
            jnp.where(rank < starts[2], bases[1] + (rank - starts[1]) * pads[1],
                      bases[2] + (rank - starts[2]) * pads[2]))
        target = jnp.sum(match * (base + running - 1.0), axis=0, keepdims=True)
        return target

    def token_matrix(g, h, target):
        target_col = jnp.broadcast_to(target, (8, length)).T[:, 0:1].astype(jnp.int32)
        to_token[g, h] = (lax.broadcasted_iota(jnp.int32, (length, slots), 1) == target_col).astype(F32).astype(BF16)

    def own_slots(h):
        target = slot_of(h)
        token_matrix(n, h, target)
        target = target.astype(jnp.int32)
        places[n, pl.ds(h, 1), :] = target
        to_slot[h] = (lax.broadcasted_iota(jnp.int32, (slots, length), 0) == target).astype(F32).astype(BF16)

    loads[3].wait()
    for c in range(2):
        w1_far[c].wait_recv()
        w1_swap[c].start()
        w1_fwd[c].start()
        if c < heads:
            own_slots(c)
    for h in range(2, heads):
        own_slots(h)
    ids_sends = [send(places.at[n], places.at[n], ids_sems.at[0, index], ids_sems.at[1, index], narrow=other)
                 for index, other in enumerate((near, far, cross))]
    for copy in ids_sends:
        copy.start()

    for part in (1, 0):
        @pl.when(me > 0)
        def _():
            halo[1 - part].wait_recv()

        attend_window(part)

    def forward(part):
        att1_sends[part][0].wait_recv()
        att1_sends[part][2].start()

    forward(3)
    forward(2)
    w1_swap[0].wait_recv()
    w1_fwd[2].start()
    forward(1)
    w1_swap[1].wait_recv()
    w1_fwd[3].start()
    for copy in loads[4:]:
        copy.wait()
    w1_near.wait_recv()
    for copy in w1_fwd:
        copy.wait_recv()

    def rest(parts):
        for part in parts:
            att1_sends[part][1].wait_recv()
            att1_sends[part][2].wait_recv()
        rows = pl.ds(parts[-1] * PIECE, len(parts) * PIECE)
        total = tokens[rows, :].astype(F32)
        for g in range(4):
            total = total + dot(att1[g, rows, :], w1[g])
        hidden16 = total.astype(BF16)
        hidden[rows, :] = hidden16
        normed2[rows, :] = rms_round(hidden16)

    rest((3, 2))
    forward(0)
    rest((1, 0))

    def place(level, head, step):
        rank = starts[level] + step
        owner = head * clusters + rank
        offset = pl.multiple_of(bases[level] + step * pads[level], 16)
        return owner, device_of(owner), offset

    def go(level, head, step):
        owner, there, offset = place(level, head, step)
        size = pads[level]
        return there, send(packed.at[head, pl.ds(offset, size)],
                           arrived.at[pl.ds(pl.multiple_of(me * size, 16), size)],
                           go_s.at[owner], go_r.at[me], wide=there), (head, offset, size)

    def each_owner(body):
        for level in range(3):
            @pl.loop(0, heads * counts[level])
            def _(item):
                body(level, lax.div(item, counts[level]), lax.rem(item, counts[level]))

    def start_go(level, head, step):
        there, copy, (_, offset, size) = go(level, head, step)

        @pl.when(there != me)
        def _():
            copy.start()

        @pl.when(there == me)
        def _():
            own = pltpu.make_async_copy(packed.at[head, pl.ds(offset, size)],
                                        arrived.at[pl.ds(pl.multiple_of(me * size, 16), size)], local_sem)
            own.start()
            own.wait()

    def leave(level, head):
        @pl.loop(0, counts[level])
        def _(step):
            start_go(level, head, step)

    order = [lax.rem(turn + jnp.where(me < wide_n // 2, 1, 0), heads) for turn in range(heads)]
    for h in order:
        packed[h] = dot(to_slot[h], dot(normed2[...], wkv2[h]).astype(BF16)).astype(BF16)
        leave(0, h)
    for level in (1, 2):
        for h in order:
            leave(level, h)

    w2_sends = []
    for index, other in enumerate((near, far, cross)):
        w2_sends.append(send(w_out2.at[:, pl.ds(pl.multiple_of(other * cols, cols), cols)], w2.at[n],
                             w2_sems.at[0, index], w2_sems.at[1, index], narrow=other))
        w2_sends[-1].start()

    for copy in ids_sends:
        copy.wait_recv()
    for g in (near, far, cross):
        for h in range(heads):
            token_matrix(g, h, places[g, pl.ds(h, 1), :].astype(F32))

    def for_level(body):
        for level in range(3):
            @pl.when((my_rank >= starts[level]) & (my_rank < starts[level] + counts[level]))
            def _():
                body(level)

    def from_source(level, source):
        size = pads[level]
        rows = pl.ds(pl.multiple_of(source * size, 16), size)
        return send(packed.at[0, pl.ds(0, size)], arrived.at[rows], go_s.at[0], go_r.at[source], wide=source)

    def back_copy(level, source):
        size = pads[level]
        rows = pl.ds(pl.multiple_of(source * size, 16), size)
        offset = pl.multiple_of(bases[level] + (my_rank - starts[level]) * size, 16)
        return rows, offset, send(answers.at[rows], ret.at[n, my_head, pl.ds(offset, size)],
                                  back_s.at[source], back_r.at[mine], wide=source)

    def receive(level, source):
        @pl.when(source != me)
        def _():
            from_source(level, source).wait_recv()

    def give_back(level, source):
        rows, offset, copy = back_copy(level, source)

        @pl.when(source != me)
        def _():
            copy.start()

        @pl.when(source == me)
        def _():
            own = pltpu.make_async_copy(answers.at[rows], ret.at[n, my_head, pl.ds(offset, pads[level])], local_sem)
            own.start()
            own.wait()

    def attend(level, block):
        size, real = pads[level], sizes[level]
        begin = block * BLOCK
        here = pl.ds(begin, BLOCK)
        q = scaled(arrived[here, pl.ds(0, HEAD_DIM)])
        value_t[:, here] = arrived[here, pl.ds(HEAD_DIM, HEAD_DIM)].T

        def score(first, rows, diagonal):
            scores = dot_nt(arrived[pl.ds(first, rows), pl.ds(0, HEAD_DIM)], q)
            keep = None
            key_at = lax.broadcasted_iota(jnp.int32, (rows, BLOCK), 0)
            if diagonal:
                query_at = lax.broadcasted_iota(jnp.int32, (rows, BLOCK), 1)
                keep = key_at < query_at
                if block == 0:
                    keep = keep | (key_at + query_at == 0)
            if size != real:
                live = lax.rem(key_at + first, size) < real
                keep = live if keep is None else keep & live
            return scores if keep is None else jnp.where(keep, scores, LOW)

        parts = [(begin, score(begin, BLOCK, True))]
        if block > 0:
            parts.append((0, score(0, begin, False)))
        top = functools.reduce(jnp.maximum, [jnp.max(scores, axis=0, keepdims=True) for _, scores in parts])
        total, mixed = 0.0, 0.0
        for first, scores in parts:
            weights = jnp.exp2(scores - top)
            total = total + jnp.sum(weights, axis=0, keepdims=True)
            mixed = mixed + dot(value_t[:, pl.ds(first, scores.shape[0])], weights.astype(BF16))
        answers[here, :] = (mixed / total).T.astype(BF16)

    def own_clusters(level):
        size = pads[level]
        came, gone = 0, 0
        for block in range(wide_n * size // BLOCK):
            end = (block + 1) * BLOCK

            @pl.loop(came, -(-end // size))
            def _(source):
                receive(level, source)

            attend(level, block)

            @pl.loop(gone, end // size)
            def _(source):
                give_back(level, source)

            came, gone = -(-end // size), end // size

    for_level(own_clusters)

    def wait_back(level, head, step):
        owner, there, offset = place(level, head, step)
        size = pads[level]

        @pl.when(there != me)
        def _():
            send(answers.at[pl.ds(0, size)], ret.at[n, head, pl.ds(offset, size)],
                 back_s.at[0], back_r.at[owner], wide=there).wait_recv()

    spans = ((0, bases[1]), (bases[1], slots - bases[1]))
    att2_sends = []
    for start, size in spans:
        for h in range(heads):
            rows = pl.ds(start, size)
            index = len(att2_sends)
            own, other = ret.at[n, h, rows], ret.at[far, h, rows]
            att2_sends.append((
                send(own, own, att2_sems.at[0, index, 0], att2_sems.at[1, index, 0], narrow=far),
                send(own, own, att2_sems.at[0, index, 1], att2_sems.at[1, index, 1], narrow=near),
                send(other, other, att2_sems.at[0, index, 2], att2_sems.at[1, index, 2], narrow=near)))
    def returned(span):
        for h in range(heads):
            for level in ((0,), (1, 2))[span]:
                @pl.loop(0, counts[level])
                def _(step):
                    wait_back(level, h, step)
            att2_sends[span * heads + h][0].start()
            att2_sends[span * heads + h][1].start()

    def pass_on(span):
        for first, second, third in att2_sends[span * heads:(span + 1) * heads]:
            first.wait_recv()
            third.start()

    @pl.when(me < wide_n // 2)
    def _():
        returned(0)
        returned(1)

    @pl.when(me >= wide_n // 2)
    def _():
        returned(1)
        pass_on(1)
        returned(0)

    def result(g):
        for half in range(length // BLOCK):
            rows = pl.ds(half * BLOCK, BLOCK)
            mixed = jnp.concatenate([dot(to_token[g, h, rows, :], ret[g, h]).astype(BF16) for h in range(heads)], axis=1)
            out[rows, :] += dot(mixed, w2[g])

    out[...] = hidden[:, mine_cols].astype(F32)
    for copy in w2_sends:
        copy.wait_recv()
    result(n)
    pass_on(0)

    @pl.when(me < wide_n // 2)
    def _():
        pass_on(1)

    for first, second, third in att2_sends:
        second.wait_recv()
    result(near)
    result(far)
    for first, second, third in att2_sends:
        third.wait_recv()
    result(cross)

    for copy in (*w1_far, w1_near, *w1_swap, *w1_fwd, *w2_sends, *ids_sends,
                 *(copy for copies in att1_sends + att2_sends for copy in copies)):
        copy.wait_send()

    @pl.when(me < wide_n - 1)
    def _():
        for copy in halo:
            copy.wait_send()

    def sent(level, head, step):
        there, copy, _ = go(level, head, step)

        @pl.when(there != me)
        def _():
            copy.wait_send()

    each_owner(sent)

    def sent_back(level):
        @pl.loop(0, wide_n)
        def _(source):
            @pl.when(source != me)
            def _():
                back_copy(level, source)[2].wait_send()

    for_level(sent_back)


def hand_on(answer, out):
    out[...] = answer[...]


def solution(mesh):
    wide_n = mesh.shape["wide"]

    def shards(tokens, w_qk1, w_value1, w_out1, w_qk2, w_value2, w_out2, cluster_ids):
        length, width = tokens.shape
        cols = w_qk1.shape[1]
        heads = cols // HEAD_DIM
        clusters = wide_n // heads
        cap = 2 * length * heads // wide_n
        sizes = (cap, 3 * cap // 8, cap // 4)
        pads = tuple(-(-size // 16) * 16 for size in sizes)
        slots = clusters // 4 * pads[0] + clusters // 2 * pads[1] + clusters // 4 * pads[2]
        most = wide_n * pads[0]
        groups = mesh.shape["narrow"]
        dma = pltpu.SemaphoreType.DMA
        vmem = pl.BlockSpec(memory_space=pltpu.VMEM)
        answer = pl.pallas_call(
            functools.partial(whole_kernel, wide_n, heads, clusters, sizes, pads, slots),
            out_shape=jax.ShapeDtypeStruct((length, cols), F32),
            in_specs=[pl.BlockSpec(memory_space=pl.ANY)] * 8,
            out_specs=vmem,
            scratch_shapes=[
                pltpu.VMEM((length, width), BF16),
                pltpu.VMEM((width, 2 * cols), BF16),
                pltpu.VMEM((heads, width, 2 * HEAD_DIM), BF16),
                pltpu.VMEM((heads, length), jnp.int32),
                pltpu.VMEM((groups, heads, length), jnp.int32),
                pltpu.VMEM((WINDOW + length, 2 * cols), BF16),
                pltpu.VMEM((groups, cols, width), BF16),
                pltpu.VMEM((groups, length, cols), BF16),
                pltpu.VMEM((length, width), BF16),
                pltpu.VMEM((length, width), BF16),
                pltpu.VMEM((heads, slots, length), BF16),
                pltpu.VMEM((groups, heads, length, slots), BF16),
                pltpu.VMEM((heads, slots, 2 * HEAD_DIM), BF16),
                pltpu.VMEM((most, 2 * HEAD_DIM), BF16),
                pltpu.VMEM((HEAD_DIM, most), BF16),
                pltpu.VMEM((most, HEAD_DIM), BF16),
                pltpu.VMEM((groups, heads, slots, HEAD_DIM), BF16),
                pltpu.VMEM((length, length), BF16),
                pltpu.VMEM((groups, cols, cols), BF16),
                dma((2, 2)), dma((2, 9)), dma((2, 4, 3)), dma((2, 3)),
                dma((wide_n,)), dma((wide_n,)), dma((wide_n,)), dma((wide_n,)),
                dma((2, 2 * heads, 3)), dma, dma((6 + 2 * heads,)), dma((2, 3)),
            ],
            compiler_params=pltpu.CompilerParams(
                collective_id=0, has_side_effects=True, vmem_limit_bytes=56 * 1024 * 1024),
        )(tokens, w_qk1, w_value1, w_out1, w_qk2, w_value2, w_out2, cluster_ids)
        return pl.pallas_call(
            hand_on,
            out_shape=jax.ShapeDtypeStruct((length, cols), F32),
            grid=(2,),
            in_specs=[pl.BlockSpec((length // 2, cols), lambda i: (i, 0))],
            out_specs=pl.BlockSpec((length // 2, cols), lambda i: (i, 0)),
        )(answer)

    placed = (
        P("wide", None),
        P(None, "narrow"),
        P(None, "narrow"),
        P("narrow", None),
        P(None, "narrow"),
        P(None, "narrow"),
        P("narrow", None),
        P("narrow", "wide"),
    )
    return jax.shard_map(
        shards, mesh=mesh, in_specs=placed, out_specs=P("wide", "narrow"), check_vma=False
    )
```
